1024 devices in a mesh: dp: 128 (over z, x), vocab: 8 (over y, core).
Axes of the slice: x: 4, y: 4, z: 32, core: 2. Of those that a mesh axis runs over, the one named last changes fastest.
Arguments:
- hidden: bfloat16 [24576, 4608], P('dp')
- table: bfloat16 [768, 4608], P('vocab')
- targets: int32 [24576], P('dp'), may hold values from 0 to 767
- loss_weight: float32 [24576], P('dp'), may hold values from 1 to 4
- token_ids: int32 [24576], P(('dp', 'vocab')), may hold values from 0 to 767, as said below
- grad_embed: bfloat16 [24576, 4608], P(('dp', 'vocab')), may hold values from -0.0234375 to 0.0234375
Outputs:
- token_loss: float32 [24576], P('dp')
- input_grad: bfloat16 [24576, 4608], P(('dp', 'vocab'))
- table_grad: bfloat16 [8, 3456, 128], P('vocab', 'dp')
The draws below stay inside these ranges and needn't reach their ends.
Inputs may be any that keep to these rules, and one draw needn't show every extreme that they name: `token_ids`: the rows of each device along dp+vocab (aligned blocks of 24) name ids of any one vocabulary block of 96 entries at most 12 times; in every group of devices along vocab all devices name exactly 12 ids of one common block.
All inputs are finite; a program needn't handle non-finite values.
Results may differ from the reference program's by a relative error of at most 0.014.
Values may be sent and summed in bfloat16 or wider, within the bound.
A program may use at most 32 MiB of HBM per device.

```python
import math
import jax
import jax.numpy as jnp
from jax import lax

D = 4608
V_DEV = 96
TOK_DEV = 192
TOKENS = 24576
VOCAB = 768
SHARDS = 8
LINES = 3456
ROWS_DEV = 24
CAP = 12


def draw_hidden(key, part):
    key = jax.random.fold_in(key, 7)
    key_noise = jax.random.fold_in(key, 0)
    values = 0.2 * jnp.clip(jax.random.normal(key_noise, (TOKENS, D)), -5.0, 5.0)
    return values.astype(jnp.bfloat16)


def draw_table(key, part):
    key = jax.random.fold_in(key, 9)
    key_noise, key_scale = jax.random.split(key, 2)
    noise = jnp.clip(jax.random.normal(key_noise, (VOCAB, D)), -4.0, 4.0)
    spread = math.log(4.0)
    position = jnp.arange(VOCAB, dtype=jnp.float32)[:, None] / VOCAB
    scales = 0.04 * jnp.exp(jax.random.uniform(key_scale, (VOCAB, 1), minval=0.0, maxval=spread))
    scales = scales * jnp.exp(position * math.log(3.0))
    return (noise * scales).astype(jnp.bfloat16)


def draw_token_ids(key, part):
    key = jax.random.fold_in(key, 5)
    key_hot, key_cold, key_order, key_first, key_second, key_perm = jax.random.split(key, 6)
    groups = TOKENS // TOK_DEV
    shape = (groups, SHARDS, ROWS_DEV)
    hot_block = jnp.broadcast_to(jax.random.randint(key_hot, (groups, 1, 1), 0, SHARDS), shape)
    cold_block = (hot_block + jax.random.randint(key_cold, shape, 1, SHARDS)) % SHARDS
    position_in = jnp.arange(ROWS_DEV, dtype=jnp.int32)[None, None, :]
    blocks = jnp.where(position_in < CAP, hot_block, cold_block)
    scores = jax.random.randint(key_order, shape, 0, 1048576) * ROWS_DEV + position_in
    row_order = jnp.argsort(scores, axis=-1, stable=True)
    blocks = jnp.take_along_axis(blocks, row_order, axis=-1)
    skewed = jnp.minimum(jax.random.randint(key_first, shape, 0, V_DEV), jax.random.randint(key_second, shape, 0, V_DEV))
    shuffle = jax.random.permutation(key_perm, V_DEV).astype(jnp.int32)
    local_id = shuffle[skewed]
    return (blocks * V_DEV + local_id).reshape(TOKENS).astype(jnp.int32)


def touch_ends(entries, stream_key, least, largest):
    shape = entries.shape
    index_at = [jax.random.randint(jax.random.fold_in(stream_key, axis), (), 0, shape[axis]) for axis in range(len(shape))]
    entries = entries.at[tuple(index_at)].set(least)
    longest = shape.index(max(shape))
    index_at[longest] = (index_at[longest] + 1) % shape[longest]
    return entries.at[tuple(index_at)].set(largest)


def levels(rng, dims, cuts, least, high):
    factor_of, own = 1.0, jax.random.fold_in(rng, 6)
    for dim, parts in cuts:
        steps = jnp.exp(jax.random.uniform(jax.random.fold_in(own, dim), (parts,), jnp.float32, least / len(cuts), high / len(cuts)))
        factor_of = factor_of * jnp.repeat(steps, dims[dim] // parts).reshape([-1 if axis == dim else 1 for axis in range(len(dims))])
    return factor_of


def centred(stream_key, shape, scale, reach, cuts=(), kind=jnp.bfloat16):
    factor_of = levels(stream_key, shape, cuts, -0.22, 0.18) if cuts else 1.0
    result = jax.random.normal(stream_key, shape, jnp.float32) * scale * factor_of
    return jnp.minimum(jnp.maximum(result, -reach), reach).astype(kind)


def setup_inputs(seed: int = 0) -> dict:
    splits = jax.random.split(jax.random.key(seed), 7)
    return {
        "hidden": draw_hidden(jax.random.fold_in(splits[6], 71), 0),
        "table": draw_table(jax.random.fold_in(splits[6], 71), 0),
        "targets": touch_ends(jax.random.randint(splits[2], (TOKENS,), 0, VOCAB), jax.random.fold_in(splits[2], 1), 0, VOCAB - 1).astype(jnp.int32),
        "loss_weight": jnp.clip(jnp.exp(math.log(4.0) - 1.3862944 * jax.random.uniform(splits[3], (TOKENS,), jnp.float32) ** levels(splits[3], (TOKENS,), ((0, 128),), -0.2, 0.2)), 1.0, 4.0),
        "token_ids": draw_token_ids(jax.random.fold_in(splits[6], 71), 0),
        "grad_embed": centred(splits[5], (TOKENS, D), 0.004, 0.0234375, ((0, 1024),)),
    }


SOFTCAP = 30.0

def reference(hidden, table, targets, loss_weight, token_ids, grad_embed):
    shards = table.reshape(SHARDS, V_DEV, D)
    indices = jnp.arange(SHARDS, dtype=jnp.int32)
    columns = jnp.arange(V_DEV, dtype=jnp.int32)

    def shard_logits(shard_index, shard_table):
        raw_logits = jnp.dot(hidden, shard_table.T, preferred_element_type=jnp.float32)
        squashed = jnp.tanh(raw_logits / SOFTCAP)
        target_hit = (targets - shard_index * V_DEV)[:, None] == columns[None, :]
        return (squashed, target_hit)

    def first_pass(shard_pair):
        squashed, target_hit = shard_logits(shard_pair[0], shard_pair[1])
        capped = SOFTCAP * squashed
        return (lax.optimization_barrier(jnp.sum(jnp.exp(capped), axis=1)), lax.optimization_barrier(jnp.sum(jnp.where(target_hit, capped, 0.0), axis=1)))
    shard_sums, picked = lax.map(first_pass, (indices, shards))
    normalizer = lax.optimization_barrier(jnp.sum(shard_sums, axis=0))
    token_loss = jnp.log(normalizer) - lax.optimization_barrier(jnp.sum(picked, axis=0))

    def second_pass(running, shard_pair):
        squashed, target_hit = shard_logits(shard_pair[0], shard_pair[1])
        probability = jnp.exp(SOFTCAP * squashed) / normalizer[:, None]
        dlogit = (loss_weight[:, None] * (probability - target_hit.astype(jnp.float32)) * (1.0 - squashed * squashed)).astype(jnp.bfloat16)
        shard_part = jnp.dot(dlogit, shard_pair[1], preferred_element_type=jnp.float32).astype(jnp.bfloat16)
        shard_part = lax.optimization_barrier(shard_part)
        head_part = jnp.dot(dlogit.T, hidden, preferred_element_type=jnp.float32)
        return (running + shard_part.astype(jnp.float32), head_part)
    summed, head_parts = lax.scan(second_pass, jnp.zeros((TOKENS, D), jnp.float32), (indices, shards))
    embed_part = jax.ops.segment_sum(grad_embed.astype(jnp.float32), token_ids, num_segments=VOCAB) * math.sqrt(D)
    table_grad = (head_parts.reshape(VOCAB, D) + embed_part).astype(jnp.bfloat16).reshape(SHARDS, LINES, 128)
    return (token_loss, summed.astype(jnp.bfloat16), table_grad)
```

```python
import functools
import math

import jax
import jax.numpy as jnp
from jax import lax
from jax.experimental import pallas as pl
from jax.experimental.pallas import tpu as pltpu
from jax.sharding import PartitionSpec as P

MESH = pl.DeviceIdType.MESH
SOFTCAP = 30.0
F32 = jnp.float32
BF16 = jnp.bfloat16

D = 4608
ENT = 96
TOK = 192
ROWS = 24
QUARTER = D // 4
PAIR = 2 * ROWS
HALF = 1792
STEP = 384
NX, NY, NZ, NC = 4, 4, 32, 2


def nt(a, b):
    return lax.dot_general(a, b, (((1,), (1,)), ((), ())), preferred_element_type=F32)


def tn(a, b):
    return lax.dot_general(a, b, (((0,), (0,)), ((), ())), preferred_element_type=F32)


def nn(a, b):
    return jnp.dot(a, b, preferred_element_type=F32)


def kernel(
    hidden_hbm, table_hbm, embed_hbm, targets_ref, weight_ref, ids_ref,
    loss_ref, input_ref, table_grad_ref,
    hid, tab, emb_in, emb, stats, xs, xown, xr, acc, ig_core, ig_core_in, ig_own, ig_y, ig_y_in,
    units, zf, zs, zr1, zb, zm, zr2,
    load_sem, emb_s, emb_r, fwd_s, fwd_r, st_s, st_r, x_s, x_r, c_s, c_r, y_s, y_r, z1_s, z1_r, z2_s, z2_r,
):
    dp = lax.axis_index("dp")
    vocab = lax.axis_index("vocab")
    z, x = dp // NX, lax.rem(dp, NX)
    y, core = vocab // NC, lax.rem(vocab, NC)
    slot = core * NY + y

    def at(dz=0, dx=0, dy=0, dc=0):
        zz, xx = lax.rem(z + dz + NZ, NZ), lax.rem(x + dx + NX, NX)
        yy, cc = lax.rem(y + dy + NY, NY), lax.rem(core + dc, NC)
        return (zz * NX + xx, yy * NC + cc)

    def remote(src, dst, send, recv, device):
        return pltpu.make_async_remote_copy(
            src_ref=src, dst_ref=dst, send_sem=send, recv_sem=recv, device_id=device, device_id_type=MESH
        )

    loads = [
        pltpu.make_async_copy(embed_hbm, emb_in, load_sem.at[0]),
        pltpu.make_async_copy(table_hbm, tab, load_sem.at[1]),
        pltpu.make_async_copy(hidden_hbm, hid, load_sem.at[2]),
    ]
    for load in loads:
        load.start()

    two = 2 - 4 * core
    near = (two, 1, -1)
    far = (4, 3, 5, 2, 6, 1, 7)
    group = [(dy, dc) for dy in (2, 1, 3, 0) for dc in range(NC) if (dy, dc) != (0, 0)]
    senders = [at(dy=dy, dc=dc) for dy, dc in group]
    senders += [at(dx=dx) for dx in (2, 1, 3)]
    senders += [at(dz=-dz) for dz in near]
    senders += [at(dz=4 * d) for d in far]
    barrier = pltpu.get_barrier_semaphore()
    for device in senders:
        pl.semaphore_signal(barrier, inc=1, device_id=device, device_id_type=MESH)

    loads[0].wait()
    row = lax.broadcasted_iota(jnp.int32, (PAIR, ROWS), 0)
    col = lax.broadcasted_iota(jnp.int32, (PAIR, ROWS), 1)
    upper = (row == col).astype(BF16)
    lower = (row == col + ROWS).astype(BF16)
    for p in range(2):
        for s in range(QUARTER // STEP):
            left = p * 2 * QUARTER + s * STEP
            placed = nn(upper, emb_in[:, left : left + STEP]) + nn(
                lower, emb_in[:, left + QUARTER : left + QUARTER + STEP]
            )
            emb[p, slot, :, s * STEP : (s + 1) * STEP] = placed.astype(BF16)

    pl.semaphore_wait(barrier, len(senders))

    emb_copies = []
    for p in range(2):
        for dy in (2, 1, 3):
            copy = remote(
                emb.at[p, slot], emb.at[p, slot], emb_s.at[p, dy - 1], emb_r.at[p, dy - 1], at(dy=dy)
            )
            copy.start()
            emb_copies.append(copy)

    loads[1].wait()
    loads[2].wait()
    squashed = jnp.tanh(nt(tab[...], hid[...]) / SOFTCAP)
    capped = SOFTCAP * squashed
    exponent = jnp.exp(capped)
    entry = lax.broadcasted_iota(jnp.int32, (ENT, TOK), 0) + vocab * ENT
    hit = entry == targets_ref[...]

    lane = lax.broadcasted_iota(jnp.int32, (1, 8 * PAIR), 1)
    place = lane - slot * PAIR
    ids_row = jnp.zeros((1, 8 * PAIR), F32)
    for r in range(ROWS):
        ids_row = jnp.where((place == r) | (place == r + ROWS), ids_ref[r].astype(F32), ids_row)
    stats[slot] = jnp.zeros((8, 8 * PAIR), F32)
    stats[slot, 0:1, 0:TOK] = jnp.sum(exponent, axis=0, keepdims=True)
    stats[slot, 1:2, 0:TOK] = jnp.sum(jnp.where(hit, capped, 0.0), axis=0, keepdims=True)
    stats[slot, 2:3, :] = ids_row
    st_copies = []
    for i, (dy, dc) in enumerate(group):
        copy = remote(stats.at[slot], stats.at[slot], st_s.at[i], st_r.at[i], at(dy=dy, dc=dc))
        copy.start()
        st_copies.append(copy)
    for copy in st_copies:
        copy.wait_recv()
    total = stats[0]
    for i in range(1, 8):
        total = total + stats[i]
    normalizer = total[0:1, 0:TOK]
    picked = total[1:2, 0:TOK]
    ids_all = total[2:3, :]
    loss_ref[...] = jnp.log(normalizer) - picked
    dlogit = (
        weight_ref[...] * (exponent / normalizer - hit.astype(F32)) * (1.0 - squashed * squashed)
    ).astype(BF16)

    def named(shape):
        i = lax.broadcasted_iota(jnp.int32, shape, 0)
        third, inner = i // 32, lax.rem(i, 32)
        cls, k = inner // 8, lax.rem(inner, 8)
        return 3 * (4 * k + cls) + third

    order = (named((ENT, ENT)) == lax.broadcasted_iota(jnp.int32, (ENT, ENT), 1)).astype(BF16)
    ordered = nn(order, dlogit).astype(BF16)
    named_id = (named((ENT, 8 * PAIR)) + vocab * ENT).astype(F32)
    is_lower = lax.rem(lax.broadcasted_iota(jnp.int32, (ENT, 8 * PAIR), 1), PAIR) >= ROWS
    match = named_id == ids_all
    wanted = [
        (match & jnp.logical_not(is_lower)).astype(BF16),
        (match & is_lower).astype(BF16),
    ]

    def forward(p):
        mine = emb.at[p, pl.ds(core * NY, NY)]
        return remote(mine, mine, fwd_s.at[p], fwd_r.at[p], at(dc=1))

    scale = math.sqrt(D)
    x_copy = lambda to, j: remote(
        xs.at[to, j],
        xr.at[lax.rem(x - to + NX, NX) - 1, j],
        x_s.at[to, j],
        x_r.at[lax.rem(x - to + NX, NX) - 1, j],
        (z * NX + to, vocab),
    )
    fwd_copies = []
    for p in range(2):
        for copy in emb_copies[3 * p : 3 * p + 3]:
            copy.wait_recv()
        copy = forward(p)
        copy.start()
        fwd_copies.append(copy)
        copy.wait_recv()
        for h in range(2):
            q = 2 * p + h
            for s in range(QUARTER // STEP):
                cols = slice(s * STEP, (s + 1) * STEP)
                rows = emb[p, :, :, cols].reshape(8 * PAIR, STEP)
                part = nn(ordered, hid[:, q * QUARTER + s * STEP : q * QUARTER + (s + 1) * STEP])
                part = part + scale * nn(wanted[h], rows)
                for r in range(3):
                    to, j = divmod(4 * r + q, 3)
                    mine = part[32 * r : 32 * (r + 1)]
                    xs[to, j, :, cols] = mine.astype(BF16)

                    @pl.when(x == to)
                    def _(mine=mine, j=j, cols=cols):
                        xown[j, :, cols] = mine

            for r in range(3):
                to, j = divmod(4 * r + q, 3)

                @pl.when(x != to)
                def _(to=to, j=j):
                    x_copy(to, j).start()

    for p in range(2):
        for s in range(QUARTER // STEP):
            left = p * 2 * QUARTER + s * STEP
            a = tn(dlogit, tab[:, left : left + STEP])
            b = tn(dlogit, tab[:, left + QUARTER : left + QUARTER + STEP])
            for v in range(8):
                take = slice(ROWS * v, ROWS * (v + 1))
                acc[p, v, :, s * STEP : (s + 1) * STEP] = jnp.concatenate([a[take], b[take]], axis=0)
    core_copies = []
    for p in range(2):
        for to in range(NY):
            ig_core[p, to] = acc[p, 2 * to + 1 - core].astype(BF16)
        copy = remote(ig_core.at[p], ig_core_in.at[p], c_s.at[p], c_r.at[p], at(dc=1))
        copy.start()
        core_copies.append(copy)

    for j in range(3):
        for d in range(3):
            remote(xs.at[0, j], xr.at[d, j], x_s.at[0, j], x_r.at[d, j], at(dx=1)).wait_recv()
        units[j] = (
            xown[j] + xr[0, j].astype(F32) + xr[1, j].astype(F32) + xr[2, j].astype(F32)
        )
    for c in range(4):
        rows = slice(8 * c, 8 * (c + 1))
        zf[c, 0:8, 0:1152] = units[0, rows, :]
        zf[c, 0:8, 1152:1792] = units[1, rows, 0:640]
        zf[c, 8:16, 0:512] = units[1, rows, 640:1152]
        zf[c, 8:16, 512:1664] = units[2, rows, :]
        zf[c, 8:16, 1664:1792] = jnp.zeros((8, 128), F32)
        zs[c] = zf[c].astype(BF16)
    z1_copies = []
    for i, dz in enumerate(near):
        copy = remote(
            zs.at[lax.rem(z + dz + 4, 4)], zr1.at[i], z1_s.at[i], z1_r.at[i], at(dz=dz)
        )
        copy.start()
        z1_copies.append(copy)

    y_copies = []
    for p in range(2):
        core_copies[p].wait_recv()
        for dy in (2, 1, 3, 0):
            to = lax.rem(y + dy, NY)
            both = acc[p, 2 * to + core] + ig_core_in[p, to].astype(F32)
            if dy == 0:
                ig_own[p] = both
            else:
                ig_y[p, dy - 1] = both.astype(BF16)
                copy = remote(
                    ig_y.at[p, dy - 1], ig_y_in.at[p, dy - 1], y_s.at[p, dy - 1], y_r.at[p, dy - 1], at(dy=dy)
                )
                copy.start()
                y_copies.append(copy)

    for copy in z1_copies:
        copy.wait_recv()
    part = (
        zf[lax.rem(z, 4)] + zr1[0].astype(F32) + zr1[1].astype(F32) + zr1[2].astype(F32)
    )
    zb[...] = jnp.zeros_like(zb)
    for line in range(27):
        up, at_line = divmod(line, 14)
        zb[:, line, :] = part[8 * up : 8 * (up + 1), 128 * at_line : 128 * (at_line + 1)]
    zm[...] = zb[...].astype(BF16)
    z2_copies = []
    for d in far:
        copy = remote(
            zm.at[lax.rem(z // 4 + d, 8)], zr2.at[d - 1], z2_s.at[d - 1], z2_r.at[d - 1], at(dz=4 * d)
        )
        copy.start()
        z2_copies.append(copy)

    for copy in y_copies:
        copy.wait_recv()
    for p in range(2):
        whole = ig_own[p]
        for i in range(3):
            whole = whole + ig_y_in[p, i].astype(F32)
        input_ref[:, p * 2 * QUARTER : p * 2 * QUARTER + QUARTER] = whole[:ROWS].astype(BF16)
        input_ref[:, p * 2 * QUARTER + QUARTER : (p + 1) * 2 * QUARTER] = whole[ROWS:].astype(BF16)

    for copy in emb_copies + fwd_copies + st_copies + core_copies + y_copies + z1_copies:
        copy.wait_send()
    for to in range(NX):
        for j in range(3):

            @pl.when(x != to)
            def _(to=to, j=j):
                x_copy(to, j).wait_send()

    for copy in z2_copies:
        copy.wait_recv()
    lines = zb[z // 4]
    for i in range(7):
        lines = lines + zr2[i].astype(F32)
    table_grad_ref[...] = lines[:27].astype(BF16)
    for copy in z2_copies:
        copy.wait_send()


def body(hidden, table, targets, loss_weight, token_ids, grad_embed):
    vmem = pl.BlockSpec(memory_space=pltpu.VMEM)
    hbm = pl.BlockSpec(memory_space=pl.ANY)
    sem = pltpu.SemaphoreType.DMA
    token_loss, input_grad, table_grad = pl.pallas_call(
        kernel,
        out_shape=(
            jax.ShapeDtypeStruct((1, TOK), F32),
            jax.ShapeDtypeStruct((ROWS, D), BF16),
            jax.ShapeDtypeStruct((27, 128), BF16),
        ),
        in_specs=[hbm, hbm, hbm, vmem, vmem, pl.BlockSpec(memory_space=pltpu.SMEM)],
        out_specs=(vmem, vmem, vmem),
        scratch_shapes=[
            pltpu.VMEM((TOK, D), BF16),
            pltpu.VMEM((ENT, D), BF16),
            pltpu.VMEM((ROWS, D), BF16),
            pltpu.VMEM((2, 8, PAIR, QUARTER), BF16),
            pltpu.VMEM((8, 8, 8 * PAIR), F32),
            pltpu.VMEM((NX, 3, 32, QUARTER), BF16),
            pltpu.VMEM((3, 32, QUARTER), F32),
            pltpu.VMEM((3, 3, 32, QUARTER), BF16),
            pltpu.VMEM((2, 8, PAIR, QUARTER), F32),
            pltpu.VMEM((2, NY, PAIR, QUARTER), BF16),
            pltpu.VMEM((2, NY, PAIR, QUARTER), BF16),
            pltpu.VMEM((2, PAIR, QUARTER), F32),
            pltpu.VMEM((2, 3, PAIR, QUARTER), BF16),
            pltpu.VMEM((2, 3, PAIR, QUARTER), BF16),
            pltpu.VMEM((3, 32, QUARTER), F32),
            pltpu.VMEM((4, 16, HALF), F32),
            pltpu.VMEM((4, 16, HALF), BF16),
            pltpu.VMEM((3, 16, HALF), BF16),
            pltpu.VMEM((8, 32, 128), F32),
            pltpu.VMEM((8, 32, 128), BF16),
            pltpu.VMEM((7, 32, 128), BF16),
            sem((3,)),
            sem((2, 3)), sem((2, 3)),
            sem((2,)), sem((2,)),
            sem((7,)), sem((7,)),
            sem((NX, 3)), sem((3, 3)),
            sem((2,)), sem((2,)),
            sem((2, 3)), sem((2, 3)),
            sem((3,)), sem((3,)),
            sem((7,)), sem((7,)),
        ],
        compiler_params=pltpu.CompilerParams(
            collective_id=0, has_side_effects=True, vmem_limit_bytes=40 * 1024 * 1024
        ),
    )(hidden, table, grad_embed, targets.reshape(1, TOK), loss_weight.reshape(1, TOK), token_ids)
    return (token_loss.reshape(TOK), input_grad, table_grad[None])


def solution(mesh):
    return jax.shard_map(
        body,
        mesh=mesh,
        in_specs=(
            P("dp", None),
            P("vocab", None),
            P("dp"),
            P("dp"),
            P(("dp", "vocab")),
            P(("dp", "vocab"), None),
        ),
        out_specs=(P("dp"), P(("dp", "vocab"), None), P("vocab", "dp", None)),
        check_vma=False,
    )
```

```python
import functools
import math

import jax
import jax.numpy as jnp
from jax import lax
from jax.experimental import pallas as pl
from jax.experimental.pallas import tpu as pltpu
from jax.sharding import PartitionSpec as P

MESH = pl.DeviceIdType.MESH
SOFTCAP = 30.0
F32 = jnp.float32
BF16 = jnp.bfloat16

D = 4608
ENT = 96
TOK = 192
ROWS = 24
QUARTER = D // 4
PAIR = 2 * ROWS
HALF = 1792
STEP = 384
NX, NY, NZ, NC = 4, 4, 32, 2


def nt(a, b):
    return lax.dot_general(a, b, (((1,), (1,)), ((), ())), preferred_element_type=F32)


def tn(a, b):
    return lax.dot_general(a, b, (((0,), (0,)), ((), ())), preferred_element_type=F32)


def nn(a, b):
    return jnp.dot(a, b, preferred_element_type=F32)


def kernel(
    hidden_hbm, table_hbm, embed_hbm, targets_hbm, weight_hbm, ids_hbm,
    loss_ref, input_ref, table_grad_ref,
    hid, tab, emb_in, targets_ref, weight_ref, ids_ref, emb, stats, xs, xown, xr, acc, ig_core, ig_core_in, ig_own, ig_y, ig_y_in,
    units, zf, zs, zr1, zb, zm, zr2,
    load_sem, in2_sem, in4_sem, in8_sem, emb_s, emb_r, fwd_s, fwd_r, st_s, st_r, x_s, x_r, c_s, c_r, y_s, y_r, z1_s, z1_r, z2_s, z2_r,
):
    dp = lax.axis_index("dp")
    vocab = lax.axis_index("vocab")
    z, x = dp // NX, lax.rem(dp, NX)
    y, core = vocab // NC, lax.rem(vocab, NC)
    slot = core * NY + y

    def at(dz=0, dx=0, dy=0, dc=0):
        zz, xx = lax.rem(z + dz + NZ, NZ), lax.rem(x + dx + NX, NX)
        yy, cc = lax.rem(y + dy + NY, NY), lax.rem(core + dc, NC)
        return (zz * NX + xx, yy * NC + cc)

    def remote(src, dst, send, recv, device):
        return pltpu.make_async_remote_copy(
            src_ref=src, dst_ref=dst, send_sem=send, recv_sem=recv, device_id=device, device_id_type=MESH
        )

    loads = [
        pltpu.make_async_copy(embed_hbm, emb_in, load_sem.at[0]),
        pltpu.make_async_copy(table_hbm, tab, load_sem.at[1]),
        pltpu.make_async_copy(hidden_hbm, hid, load_sem.at[2]),
        pltpu.make_async_copy(targets_hbm, targets_ref, load_sem.at[3]),
        pltpu.make_async_copy(weight_hbm, weight_ref, load_sem.at[4]),
        pltpu.make_async_copy(ids_hbm, ids_ref, load_sem.at[5]),
    ]
    for load in loads:
        load.start()

    two = 2 - 4 * core
    near = (two, 1, -1)
    far = (4, 3, 5, 2, 6, 1, 7)
    group = [(dy, dc) for dy in (2, 1, 3, 0) for dc in range(NC) if (dy, dc) != (0, 0)]
    greeted = [at(dy=dy, dc=dc) for dy, dc in group]
    greeted += [at(dx=dx) for dx in (2, 1, 3)]
    greeted += [at(dz=dz) for dz in (1, -1, 2, -2)]
    barrier = pltpu.get_barrier_semaphore()
    for device in greeted:
        pl.semaphore_signal(barrier, inc=1, device_id=device, device_id_type=MESH)

    loads[0].wait()
    row = lax.broadcasted_iota(jnp.int32, (PAIR, ROWS), 0)
    col = lax.broadcasted_iota(jnp.int32, (PAIR, ROWS), 1)
    upper = (row == col).astype(BF16)
    lower = (row == col + ROWS).astype(BF16)
    for p in range(2):
        for s in range(QUARTER // STEP):
            left = p * 2 * QUARTER + s * STEP
            placed = nn(upper, emb_in[:, left : left + STEP]) + nn(
                lower, emb_in[:, left + QUARTER : left + QUARTER + STEP]
            )
            emb[p, slot, :, s * STEP : (s + 1) * STEP] = placed.astype(BF16)

    pl.semaphore_wait(barrier, len(greeted))

    def pass_on(reach, heard):
        for dz in (reach, -reach):
            pl.semaphore_signal(heard, inc=1, device_id=at(dz=dz), device_id_type=MESH)

    emb_copies = []

    def send_rows(p):
        for dy in (2, 1, 3):
            copy = remote(
                emb.at[p, slot], emb.at[p, slot], emb_s.at[p, dy - 1], emb_r.at[p, dy - 1], at(dy=dy)
            )
            copy.start()
            emb_copies.append(copy)

    send_rows(0)
    pass_on(2, in2_sem)

    loads[1].wait()
    for load in loads[2:]:
        load.wait()
    squashed = jnp.tanh(nt(tab[...], hid[...]) / SOFTCAP)
    capped = SOFTCAP * squashed
    exponent = jnp.exp(capped)
    entry = lax.broadcasted_iota(jnp.int32, (ENT, TOK), 0) + vocab * ENT
    hit = entry == targets_ref[...]

    lane = lax.broadcasted_iota(jnp.int32, (1, 8 * PAIR), 1)
    place = lane - slot * PAIR
    ids_row = jnp.zeros((1, 8 * PAIR), F32)
    for r in range(ROWS):
        ids_row = jnp.where((place == r) | (place == r + ROWS), ids_ref[r].astype(F32), ids_row)
    stats[slot] = jnp.zeros((8, 8 * PAIR), F32)
    stats[slot, 0:1, 0:TOK] = jnp.sum(exponent, axis=0, keepdims=True)
    stats[slot, 1:2, 0:TOK] = jnp.sum(jnp.where(hit, capped, 0.0), axis=0, keepdims=True)
    stats[slot, 2:3, :] = ids_row
    st_copies = []
    for i, (dy, dc) in enumerate(group):
        copy = remote(stats.at[slot], stats.at[slot], st_s.at[i], st_r.at[i], at(dy=dy, dc=dc))
        copy.start()
        st_copies.append(copy)
    send_rows(1)
    for copy in st_copies:
        copy.wait_recv()
    total = stats[0]
    for i in range(1, 8):
        total = total + stats[i]
    normalizer = total[0:1, 0:TOK]
    picked = total[1:2, 0:TOK]
    ids_all = total[2:3, :]
    loss_ref[...] = jnp.log(normalizer) - picked
    dlogit = (
        weight_ref[...] * (exponent / normalizer - hit.astype(F32)) * (1.0 - squashed * squashed)
    ).astype(BF16)

    pl.semaphore_wait(in2_sem, 2)
    pass_on(4, in4_sem)

    def named(shape):
        i = lax.broadcasted_iota(jnp.int32, shape, 0)
        third, inner = i // 32, lax.rem(i, 32)
        cls, k = inner // 8, lax.rem(inner, 8)
        return 3 * (4 * k + cls) + third

    order = (named((ENT, ENT)) == lax.broadcasted_iota(jnp.int32, (ENT, ENT), 1)).astype(BF16)
    ordered = nn(order, dlogit).astype(BF16)
    named_id = (named((ENT, 8 * PAIR)) + vocab * ENT).astype(F32)
    is_lower = lax.rem(lax.broadcasted_iota(jnp.int32, (ENT, 8 * PAIR), 1), PAIR) >= ROWS
    match = named_id == ids_all
    wanted = [
        (match & jnp.logical_not(is_lower)).astype(BF16),
        (match & is_lower).astype(BF16),
    ]

    def forward(p):
        mine = emb.at[p, pl.ds(core * NY, NY)]
        return remote(mine, mine, fwd_s.at[p], fwd_r.at[p], at(dc=1))

    scale = math.sqrt(D)
    x_copy = lambda to, j: remote(
        xs.at[to, j],
        xr.at[lax.rem(x - to + NX, NX) - 1, j],
        x_s.at[to, j],
        x_r.at[lax.rem(x - to + NX, NX) - 1, j],
        (z * NX + to, vocab),
    )
    fwd_copies = []
    for p in range(2):
        for copy in emb_copies[3 * p : 3 * p + 3]:
            copy.wait_recv()
        copy = forward(p)
        copy.start()
        fwd_copies.append(copy)
        copy.wait_recv()
        for h in range(2):
            q = 2 * p + h
            for s in range(QUARTER // STEP):
                cols = slice(s * STEP, (s + 1) * STEP)
                rows = emb[p, :, :, cols].reshape(8 * PAIR, STEP)
                part = nn(ordered, hid[:, q * QUARTER + s * STEP : q * QUARTER + (s + 1) * STEP])
                part = part + scale * nn(wanted[h], rows)
                for r in range(3):
                    to, j = divmod(4 * r + q, 3)
                    mine = part[32 * r : 32 * (r + 1)]
                    xs[to, j, :, cols] = mine.astype(BF16)

                    @pl.when(x == to)
                    def _(mine=mine, j=j, cols=cols):
                        xown[j, :, cols] = mine

            for r in range(3):
                to, j = divmod(4 * r + q, 3)

                @pl.when(x != to)
                def _(to=to, j=j):
                    x_copy(to, j).start()

    for p in range(2):
        for s in range(QUARTER // STEP):
            left = p * 2 * QUARTER + s * STEP
            a = tn(dlogit, tab[:, left : left + STEP])
            b = tn(dlogit, tab[:, left + QUARTER : left + QUARTER + STEP])
            for v in range(8):
                take = slice(ROWS * v, ROWS * (v + 1))
                acc[p, v, :, s * STEP : (s + 1) * STEP] = jnp.concatenate([a[take], b[take]], axis=0)
    core_copies = []
    for p in range(2):
        for to in range(NY):
            ig_core[p, to] = acc[p, 2 * to + 1 - core].astype(BF16)
        copy = remote(ig_core.at[p], ig_core_in.at[p], c_s.at[p], c_r.at[p], at(dc=1))
        copy.start()
        core_copies.append(copy)

    pl.semaphore_wait(in4_sem, 2)
    pass_on(8, in8_sem)

    for j in range(3):
        for d in range(3):
            remote(xs.at[0, j], xr.at[d, j], x_s.at[0, j], x_r.at[d, j], at(dx=1)).wait_recv()
        units[j] = (
            xown[j] + xr[0, j].astype(F32) + xr[1, j].astype(F32) + xr[2, j].astype(F32)
        )
    for c in range(4):
        rows = slice(8 * c, 8 * (c + 1))
        zf[c, 0:8, 0:1152] = units[0, rows, :]
        zf[c, 0:8, 1152:1792] = units[1, rows, 0:640]
        zf[c, 8:16, 0:512] = units[1, rows, 640:1152]
        zf[c, 8:16, 512:1664] = units[2, rows, :]
        zf[c, 8:16, 1664:1792] = jnp.zeros((8, 128), F32)
        zs[c] = zf[c].astype(BF16)
    z1_copies = []
    for i, dz in enumerate(near):
        copy = remote(
            zs.at[lax.rem(z + dz + 4, 4)], zr1.at[i], z1_s.at[i], z1_r.at[i], at(dz=dz)
        )
        copy.start()
        z1_copies.append(copy)

    y_copies = []
    for p in range(2):
        core_copies[p].wait_recv()
        for dy in (2, 1, 3, 0):
            to = lax.rem(y + dy, NY)
            both = acc[p, 2 * to + core] + ig_core_in[p, to].astype(F32)
            if dy == 0:
                ig_own[p] = both
            else:
                ig_y[p, dy - 1] = both.astype(BF16)
                copy = remote(
                    ig_y.at[p, dy - 1], ig_y_in.at[p, dy - 1], y_s.at[p, dy - 1], y_r.at[p, dy - 1], at(dy=dy)
                )
                copy.start()
                y_copies.append(copy)

    for copy in z1_copies:
        copy.wait_recv()
    part = (
        zf[lax.rem(z, 4)] + zr1[0].astype(F32) + zr1[1].astype(F32) + zr1[2].astype(F32)
    )
    zb[...] = jnp.zeros_like(zb)
    for line in range(27):
        up, at_line = divmod(line, 14)
        zb[:, line, :] = part[8 * up : 8 * (up + 1), 128 * at_line : 128 * (at_line + 1)]
    zm[...] = zb[...].astype(BF16)
    pl.semaphore_wait(in8_sem, 2)
    z2_copies = []
    for d in far:
        copy = remote(
            zm.at[lax.rem(z // 4 + d, 8)], zr2.at[d - 1], z2_s.at[d - 1], z2_r.at[d - 1], at(dz=4 * d)
        )
        copy.start()
        z2_copies.append(copy)

    for copy in y_copies:
        copy.wait_recv()
    for p in range(2):
        whole = ig_own[p]
        for i in range(3):
            whole = whole + ig_y_in[p, i].astype(F32)
        input_ref[:, p * 2 * QUARTER : p * 2 * QUARTER + QUARTER] = whole[:ROWS].astype(BF16)
        input_ref[:, p * 2 * QUARTER + QUARTER : (p + 1) * 2 * QUARTER] = whole[ROWS:].astype(BF16)

    for copy in emb_copies + fwd_copies + st_copies + core_copies + y_copies + z1_copies:
        copy.wait_send()
    for to in range(NX):
        for j in range(3):

            @pl.when(x != to)
            def _(to=to, j=j):
                x_copy(to, j).wait_send()

    for copy in z2_copies:
        copy.wait_recv()
    lines = zb[z // 4]
    for i in range(7):
        lines = lines + zr2[i].astype(F32)
    table_grad_ref[...] = lines[:27].astype(BF16)
    for copy in z2_copies:
        copy.wait_send()


def body(hidden, table, targets, loss_weight, token_ids, grad_embed):
    vmem = pl.BlockSpec(memory_space=pltpu.VMEM)
    hbm = pl.BlockSpec(memory_space=pl.ANY)
    sem = pltpu.SemaphoreType.DMA
    token_loss, input_grad, table_grad = pl.pallas_call(
        kernel,
        out_shape=(
            jax.ShapeDtypeStruct((1, TOK), F32),
            jax.ShapeDtypeStruct((ROWS, D), BF16),
            jax.ShapeDtypeStruct((27, 128), BF16),
        ),
        in_specs=[hbm] * 6,
        out_specs=(vmem, vmem, vmem),
        scratch_shapes=[
            pltpu.VMEM((TOK, D), BF16),
            pltpu.VMEM((ENT, D), BF16),
            pltpu.VMEM((ROWS, D), BF16),
            pltpu.VMEM((1, TOK), jnp.int32),
            pltpu.VMEM((1, TOK), F32),
            pltpu.SMEM((ROWS,), jnp.int32),
            pltpu.VMEM((2, 8, PAIR, QUARTER), BF16),
            pltpu.VMEM((8, 8, 8 * PAIR), F32),
            pltpu.VMEM((NX, 3, 32, QUARTER), BF16),
            pltpu.VMEM((3, 32, QUARTER), F32),
            pltpu.VMEM((3, 3, 32, QUARTER), BF16),
            pltpu.VMEM((2, 8, PAIR, QUARTER), F32),
            pltpu.VMEM((2, NY, PAIR, QUARTER), BF16),
            pltpu.VMEM((2, NY, PAIR, QUARTER), BF16),
            pltpu.VMEM((2, PAIR, QUARTER), F32),
            pltpu.VMEM((2, 3, PAIR, QUARTER), BF16),
            pltpu.VMEM((2, 3, PAIR, QUARTER), BF16),
            pltpu.VMEM((3, 32, QUARTER), F32),
            pltpu.VMEM((4, 16, HALF), F32),
            pltpu.VMEM((4, 16, HALF), BF16),
            pltpu.VMEM((3, 16, HALF), BF16),
            pltpu.VMEM((8, 32, 128), F32),
            pltpu.VMEM((8, 32, 128), BF16),
            pltpu.VMEM((7, 32, 128), BF16),
            sem((6,)),
            pltpu.SemaphoreType.REGULAR, pltpu.SemaphoreType.REGULAR, pltpu.SemaphoreType.REGULAR,
            sem((2, 3)), sem((2, 3)),
            sem((2,)), sem((2,)),
            sem((7,)), sem((7,)),
            sem((NX, 3)), sem((3, 3)),
            sem((2,)), sem((2,)),
            sem((2, 3)), sem((2, 3)),
            sem((3,)), sem((3,)),
            sem((7,)), sem((7,)),
        ],
        compiler_params=pltpu.CompilerParams(
            collective_id=0, has_side_effects=True, vmem_limit_bytes=56 * 1024 * 1024
        ),
    )(hidden, table, grad_embed, targets.reshape(1, TOK), loss_weight.reshape(1, TOK), token_ids)
    return (token_loss.reshape(TOK), input_grad, table_grad[None])


def solution(mesh):
    return jax.shard_map(
        body,
        mesh=mesh,
        in_specs=(
            P("dp", None),
            P("vocab", None),
            P("dp"),
            P("dp"),
            P(("dp", "vocab")),
            P(("dp", "vocab"), None),
        ),
        out_specs=(P("dp"), P(("dp", "vocab"), None), P("vocab", "dp", None)),
        check_vma=False,
    )
```

```python
import functools
import math

import jax
import jax.numpy as jnp
from jax import lax
from jax.experimental import pallas as pl
from jax.experimental.pallas import tpu as pltpu
from jax.sharding import PartitionSpec as P

MESH = pl.DeviceIdType.MESH
SOFTCAP = 30.0
F32 = jnp.float32
BF16 = jnp.bfloat16

D = 4608
ENT = 96
TOK = 192
ROWS = 24
QUARTER = D // 4
PAIR = 2 * ROWS
PART_A = 640
PART_B = QUARTER - PART_A
HALF = 1024
STEP = 384
NX, NY, NZ, NC = 4, 4, 32, 2


def nt(a, b):
    return lax.dot_general(a, b, (((1,), (1,)), ((), ())), preferred_element_type=F32)


def tn(a, b):
    return lax.dot_general(a, b, (((0,), (0,)), ((), ())), preferred_element_type=F32)


def nn(a, b):
    return jnp.dot(a, b, preferred_element_type=F32)


def kernel(
    hidden_hbm, table_hbm, embed_hbm, targets_hbm, weight_hbm, ids_hbm,
    loss_ref, input_ref, table_grad_ref,
    hid, tab, emb_in, targets_ref, weight_ref, ids_ref, emb, stats, xs, xown, xr, acc, ig_core, ig_core_in, ig_own, ig_y, ig_y_in,
    units, zf, zs, zr1, bf, bs, br1, b2f, b2, b2r, zb, zm, zr2,
    load_sem, in2_sem, in4_sem, in8_sem, emb_s, emb_r, fwd_s, fwd_r, st_s, st_r, x_s, x_r, c_s, c_r, y_s, y_r, z1_s, z1_r, b1_s, b1_r, b2_s, b2_r, z2_s, z2_r,
):
    dp = lax.axis_index("dp")
    vocab = lax.axis_index("vocab")
    z, x = dp // NX, lax.rem(dp, NX)
    y, core = vocab // NC, lax.rem(vocab, NC)
    slot = core * NY + y

    def at(dz=0, dx=0, dy=0, dc=0):
        zz, xx = lax.rem(z + dz + NZ, NZ), lax.rem(x + dx + NX, NX)
        yy, cc = lax.rem(y + dy + NY, NY), lax.rem(core + dc, NC)
        return (zz * NX + xx, yy * NC + cc)

    def remote(src, dst, send, recv, device):
        return pltpu.make_async_remote_copy(
            src_ref=src, dst_ref=dst, send_sem=send, recv_sem=recv, device_id=device, device_id_type=MESH
        )

    loads = [
        pltpu.make_async_copy(embed_hbm, emb_in, load_sem.at[0]),
        pltpu.make_async_copy(table_hbm, tab, load_sem.at[1]),
        pltpu.make_async_copy(hidden_hbm, hid, load_sem.at[2]),
        pltpu.make_async_copy(targets_hbm, targets_ref, load_sem.at[3]),
        pltpu.make_async_copy(weight_hbm, weight_ref, load_sem.at[4]),
        pltpu.make_async_copy(ids_hbm, ids_ref, load_sem.at[5]),
    ]
    for load in loads:
        load.start()

    two = 2 - 4 * core
    near = (two, 1, -1)
    far = (4, 3, 5, 2, 6, 1, 7)
    group = [(dy, dc) for dy in (2, 1, 3, 0) for dc in range(NC) if (dy, dc) != (0, 0)]
    greeted = [at(dy=dy, dc=dc) for dy, dc in group]
    greeted += [at(dx=dx) for dx in (2, 1, 3)]
    greeted += [at(dz=dz) for dz in (1, -1, 2, -2)]
    barrier = pltpu.get_barrier_semaphore()
    for device in greeted:
        pl.semaphore_signal(barrier, inc=1, device_id=device, device_id_type=MESH)

    loads[0].wait()
    row = lax.broadcasted_iota(jnp.int32, (PAIR, ROWS), 0)
    col = lax.broadcasted_iota(jnp.int32, (PAIR, ROWS), 1)
    upper = (row == col).astype(BF16)
    lower = (row == col + ROWS).astype(BF16)
    for p in range(2):
        for s in range(QUARTER // STEP):
            left = p * 2 * QUARTER + s * STEP
            placed = nn(upper, emb_in[:, left : left + STEP]) + nn(
                lower, emb_in[:, left + QUARTER : left + QUARTER + STEP]
            )
            emb[p, slot, :, s * STEP : (s + 1) * STEP] = placed.astype(BF16)

    pl.semaphore_wait(barrier, len(greeted))

    def pass_on(reach, heard):
        for dz in (reach, -reach):
            pl.semaphore_signal(heard, inc=1, device_id=at(dz=dz), device_id_type=MESH)

    emb_copies = []

    def send_rows(p):
        for dy in (2, 1, 3):
            copy = remote(
                emb.at[p, slot], emb.at[p, slot], emb_s.at[p, dy - 1], emb_r.at[p, dy - 1], at(dy=dy)
            )
            copy.start()
            emb_copies.append(copy)

    send_rows(0)
    pass_on(2, in2_sem)

    loads[1].wait()
    for load in loads[2:]:
        load.wait()
    squashed = jnp.tanh(nt(tab[...], hid[...]) / SOFTCAP)
    capped = SOFTCAP * squashed
    exponent = jnp.exp(capped)
    entry = lax.broadcasted_iota(jnp.int32, (ENT, TOK), 0) + vocab * ENT
    hit = entry == targets_ref[...]

    lane = lax.broadcasted_iota(jnp.int32, (1, 8 * PAIR), 1)
    place = lane - slot * PAIR
    ids_row = jnp.zeros((1, 8 * PAIR), F32)
    for r in range(ROWS):
        ids_row = jnp.where((place == r) | (place == r + ROWS), ids_ref[r].astype(F32), ids_row)
    stats[slot] = jnp.zeros((8, 8 * PAIR), F32)
    stats[slot, 0:1, 0:TOK] = jnp.sum(exponent, axis=0, keepdims=True)
    stats[slot, 1:2, 0:TOK] = jnp.sum(jnp.where(hit, capped, 0.0), axis=0, keepdims=True)
    stats[slot, 2:3, :] = ids_row
    st_copies = []
    for i, (dy, dc) in enumerate(group):
        copy = remote(stats.at[slot], stats.at[slot], st_s.at[i], st_r.at[i], at(dy=dy, dc=dc))
        copy.start()
        st_copies.append(copy)
    send_rows(1)
    pl.semaphore_wait(in2_sem, 2)
    pass_on(4, in4_sem)
    for copy in st_copies:
        copy.wait_recv()
    total = stats[0]
    for i in range(1, 8):
        total = total + stats[i]
    normalizer = total[0:1, 0:TOK]
    picked = total[1:2, 0:TOK]
    ids_all = total[2:3, :]
    loss_ref[...] = jnp.log(normalizer) - picked
    dlogit = (
        weight_ref[...] * (exponent / normalizer - hit.astype(F32)) * (1.0 - squashed * squashed)
    ).astype(BF16)

    def named(shape):
        i = lax.broadcasted_iota(jnp.int32, shape, 0)
        third, inner = i // 32, lax.rem(i, 32)
        cls, k = inner // 8, lax.rem(inner, 8)
        return 3 * (4 * k + cls) + third

    order = (named((ENT, ENT)) == lax.broadcasted_iota(jnp.int32, (ENT, ENT), 1)).astype(BF16)
    ordered = nn(order, dlogit).astype(BF16)
    named_id = (named((ENT, 8 * PAIR)) + vocab * ENT).astype(F32)
    is_lower = lax.rem(lax.broadcasted_iota(jnp.int32, (ENT, 8 * PAIR), 1), PAIR) >= ROWS
    match = named_id == ids_all
    wanted = [
        (match & jnp.logical_not(is_lower)).astype(BF16),
        (match & is_lower).astype(BF16),
    ]

    def forward(p):
        mine = emb.at[p, pl.ds(core * NY, NY)]
        return remote(mine, mine, fwd_s.at[p], fwd_r.at[p], at(dc=1))

    scale = math.sqrt(D)
    x_copy = lambda to, j: remote(
        xs.at[to, j],
        xr.at[lax.rem(x - to + NX, NX) - 1, j],
        x_s.at[to, j],
        x_r.at[lax.rem(x - to + NX, NX) - 1, j],
        (z * NX + to, vocab),
    )
    fwd_copies = []
    b1_copies = []
    for p in range(2):
        for copy in emb_copies[3 * p : 3 * p + 3]:
            copy.wait_recv()
        copy = forward(p)
        copy.start()
        fwd_copies.append(copy)
        copy.wait_recv()
        for h in range(2):
            q = 2 * p + h
            for lo, hi in ((0, 384), (384, PART_A), (PART_A, QUARTER)):
                rows = emb[p, :, :, lo:hi].reshape(8 * PAIR, hi - lo)
                part = nn(ordered, hid[:, q * QUARTER + lo : q * QUARTER + hi])
                part = part + scale * nn(wanted[h], rows)
                for r in range(3):
                    if lo == PART_A:
                        for c in range(4):
                            eight = part[32 * r + 8 * c : 32 * r + 8 * (c + 1)]
                            folded = jnp.concatenate([eight[:, : PART_B // 2], eight[:, PART_B // 2 :]], axis=0)
                            bf[c, p, 2 * r + h] = folded
                            bs[c, p, 2 * r + h] = folded.astype(BF16)
                        continue
                    to, j = divmod(4 * r + q, 3)
                    mine = part[32 * r : 32 * (r + 1)]
                    xs[to, j, :, lo:hi] = mine.astype(BF16)

                    @pl.when(x == to)
                    def _(mine=mine, j=j, lo=lo, hi=hi):
                        xown[j, :, lo:hi] = mine

            for r in range(3):
                to, j = divmod(4 * r + q, 3)

                @pl.when(x != to)
                def _(to=to, j=j):
                    x_copy(to, j).start()

        for i, dz in enumerate(near):
            copy = remote(
                bs.at[lax.rem(z + dz + 4, 4), p], br1.at[i, p], b1_s.at[i, p], b1_r.at[i, p], at(dz=dz)
            )
            copy.start()
            b1_copies.append(copy)

    pl.semaphore_wait(in4_sem, 2)
    pass_on(8, in8_sem)

    for p in range(2):
        for s in range(QUARTER // STEP):
            left = p * 2 * QUARTER + s * STEP
            a = tn(dlogit, tab[:, left : left + STEP])
            b = tn(dlogit, tab[:, left + QUARTER : left + QUARTER + STEP])
            for v in range(8):
                take = slice(ROWS * v, ROWS * (v + 1))
                acc[p, v, :, s * STEP : (s + 1) * STEP] = jnp.concatenate([a[take], b[take]], axis=0)
    core_copies = []
    for p in range(2):
        for to in range(NY):
            ig_core[p, to] = acc[p, 2 * to + 1 - core].astype(BF16)
        copy = remote(ig_core.at[p], ig_core_in.at[p], c_s.at[p], c_r.at[p], at(dc=1))
        copy.start()
        core_copies.append(copy)

    for j in range(3):
        for d in range(3):
            remote(xs.at[0, j], xr.at[d, j], x_s.at[0, j], x_r.at[d, j], at(dx=1)).wait_recv()
        units[j] = (
            xown[j] + xr[0, j].astype(F32) + xr[1, j].astype(F32) + xr[2, j].astype(F32)
        )
    for c in range(4):
        rows = slice(8 * c, 8 * (c + 1))
        zf[c, 0:8, 0:640] = units[0, rows, :]
        zf[c, 0:8, 640:1024] = units[1, rows, 0:384]
        zf[c, 8:16, 0:256] = units[1, rows, 384:640]
        zf[c, 8:16, 256:896] = units[2, rows, :]
        zf[c, 8:16, 896:1024] = jnp.zeros((8, 128), F32)
        zs[c] = zf[c].astype(BF16)
    z1_copies = []
    for i, dz in enumerate(near):
        copy = remote(
            zs.at[lax.rem(z + dz + 4, 4)], zr1.at[i], z1_s.at[i], z1_r.at[i], at(dz=dz)
        )
        copy.start()
        z1_copies.append(copy)

    for copy in b1_copies:
        copy.wait_recv()
    for p in range(2):
        for i in range(6):
            r, h = divmod(i, 2)
            to, j = divmod(4 * r + 2 * p + h, 3)
            four = bf[lax.rem(z, 4), p, i]
            for n in range(3):
                four = four + br1[n, p, i].astype(F32)
            b2f[to, j] = four
            b2[to, j] = four.astype(BF16)
    b2_copies = []
    for i, dx in enumerate((1, 2, 3)):
        copy = remote(b2.at[lax.rem(x + dx, NX)], b2r.at[i], b2_s.at[i], b2_r.at[i], at(dx=dx))
        copy.start()
        b2_copies.append(copy)

    y_copies = []
    for p in range(2):
        core_copies[p].wait_recv()
        for dy in (2, 1, 3, 0):
            to = lax.rem(y + dy, NY)
            both = acc[p, 2 * to + core] + ig_core_in[p, to].astype(F32)
            if dy == 0:
                ig_own[p] = both
            else:
                ig_y[p, dy - 1] = both.astype(BF16)
                copy = remote(
                    ig_y.at[p, dy - 1], ig_y_in.at[p, dy - 1], y_s.at[p, dy - 1], y_r.at[p, dy - 1], at(dy=dy)
                )
                copy.start()
                y_copies.append(copy)

    for copy in z1_copies + b2_copies:
        copy.wait_recv()
    part = (
        zf[lax.rem(z, 4)] + zr1[0].astype(F32) + zr1[1].astype(F32) + zr1[2].astype(F32)
    )
    zb[...] = jnp.zeros_like(zb)
    for j in range(3):
        lower_part = b2f[x, j]
        for n in range(3):
            lower_part = lower_part + b2r[n, j].astype(F32)
        for line in range(5):
            up, at_line = divmod(5 * j + line, 8)
            zb[:, 9 * j + line, :] = part[8 * up : 8 * (up + 1), 128 * at_line : 128 * (at_line + 1)]
        for line in range(4):
            up, at_line = divmod(line, 2)
            zb[:, 9 * j + 5 + line, :] = lower_part[8 * up : 8 * (up + 1), 128 * at_line : 128 * (at_line + 1)]
    zm[...] = zb[...].astype(BF16)
    pl.semaphore_wait(in8_sem, 2)
    z2_copies = []
    for d in far:
        copy = remote(
            zm.at[lax.rem(z // 4 + d, 8)], zr2.at[d - 1], z2_s.at[d - 1], z2_r.at[d - 1], at(dz=4 * d)
        )
        copy.start()
        z2_copies.append(copy)

    for copy in y_copies:
        copy.wait_recv()
    for p in range(2):
        whole = ig_own[p]
        for i in range(3):
            whole = whole + ig_y_in[p, i].astype(F32)
        input_ref[:, p * 2 * QUARTER : p * 2 * QUARTER + QUARTER] = whole[:ROWS].astype(BF16)
        input_ref[:, p * 2 * QUARTER + QUARTER : (p + 1) * 2 * QUARTER] = whole[ROWS:].astype(BF16)

    for copy in emb_copies + fwd_copies + st_copies + core_copies + y_copies + z1_copies + b1_copies + b2_copies:
        copy.wait_send()
    for to in range(NX):
        for j in range(3):

            @pl.when(x != to)
            def _(to=to, j=j):
                x_copy(to, j).wait_send()

    for copy in z2_copies:
        copy.wait_recv()
    lines = zb[z // 4]
    for i in range(7):
        lines = lines + zr2[i].astype(F32)
    table_grad_ref[...] = lines[:27].astype(BF16)
    for copy in z2_copies:
        copy.wait_send()


def hand_over(a, b, c, a_out, b_out, c_out, a_mid, b_mid, c_mid, in_sem, out_sem):
    arrive = [
        pltpu.make_async_copy(src, mid, in_sem.at[i])
        for i, (src, mid) in enumerate(((a, a_mid), (b, b_mid), (c, c_mid)))
    ]
    leave = [
        pltpu.make_async_copy(mid, dst, out_sem.at[i])
        for i, (mid, dst) in enumerate(((a_mid, a_out), (b_mid, b_out), (c_mid, c_out)))
    ]
    for copy in arrive:
        copy.start()
    for come, go in zip(arrive, leave):
        come.wait()
        go.start()
    for copy in leave:
        copy.wait()


def body(hidden, table, targets, loss_weight, token_ids, grad_embed):
    vmem = pl.BlockSpec(memory_space=pltpu.VMEM)
    hbm = pl.BlockSpec(memory_space=pl.ANY)
    sem = pltpu.SemaphoreType.DMA
    results = pl.pallas_call(
        kernel,
        out_shape=(
            jax.ShapeDtypeStruct((1, TOK), F32),
            jax.ShapeDtypeStruct((ROWS, D), BF16),
            jax.ShapeDtypeStruct((27, 128), BF16),
        ),
        in_specs=[hbm] * 6,
        out_specs=(vmem, vmem, vmem),
        scratch_shapes=[
            pltpu.VMEM((TOK, D), BF16),
            pltpu.VMEM((ENT, D), BF16),
            pltpu.VMEM((ROWS, D), BF16),
            pltpu.VMEM((1, TOK), jnp.int32),
            pltpu.VMEM((1, TOK), F32),
            pltpu.SMEM((ROWS,), jnp.int32),
            pltpu.VMEM((2, 8, PAIR, QUARTER), BF16),
            pltpu.VMEM((8, 8, 8 * PAIR), F32),
            pltpu.VMEM((NX, 3, 32, PART_A), BF16),
            pltpu.VMEM((3, 32, PART_A), F32),
            pltpu.VMEM((3, 3, 32, PART_A), BF16),
            pltpu.VMEM((2, 8, PAIR, QUARTER), F32),
            pltpu.VMEM((2, NY, PAIR, QUARTER), BF16),
            pltpu.VMEM((2, NY, PAIR, QUARTER), BF16),
            pltpu.VMEM((2, PAIR, QUARTER), F32),
            pltpu.VMEM((2, 3, PAIR, QUARTER), BF16),
            pltpu.VMEM((2, 3, PAIR, QUARTER), BF16),
            pltpu.VMEM((3, 32, PART_A), F32),
            pltpu.VMEM((4, 16, HALF), F32),
            pltpu.VMEM((4, 16, HALF), BF16),
            pltpu.VMEM((3, 16, HALF), BF16),
            pltpu.VMEM((4, 2, 6, 16, PART_B // 2), F32),
            pltpu.VMEM((4, 2, 6, 16, PART_B // 2), BF16),
            pltpu.VMEM((3, 2, 6, 16, PART_B // 2), BF16),
            pltpu.VMEM((NX, 3, 16, PART_B // 2), F32),
            pltpu.VMEM((NX, 3, 16, PART_B // 2), BF16),
            pltpu.VMEM((3, 3, 16, PART_B // 2), BF16),
            pltpu.VMEM((8, 32, 128), F32),
            pltpu.VMEM((8, 32, 128), BF16),
            pltpu.VMEM((7, 32, 128), BF16),
            sem((6,)),
            pltpu.SemaphoreType.REGULAR, pltpu.SemaphoreType.REGULAR, pltpu.SemaphoreType.REGULAR,
            sem((2, 3)), sem((2, 3)),
            sem((2,)), sem((2,)),
            sem((7,)), sem((7,)),
            sem((NX, 3)), sem((3, 3)),
            sem((2,)), sem((2,)),
            sem((2, 3)), sem((2, 3)),
            sem((3,)), sem((3,)),
            sem((3, 2)), sem((3, 2)),
            sem((3,)), sem((3,)),
            sem((7,)), sem((7,)),
        ],
        compiler_params=pltpu.CompilerParams(
            collective_id=0, has_side_effects=True, vmem_limit_bytes=56 * 1024 * 1024
        ),
    )(hidden, table, grad_embed, targets.reshape(1, TOK), loss_weight.reshape(1, TOK), token_ids)
    token_loss, input_grad, table_grad = pl.pallas_call(
        hand_over,
        out_shape=tuple(jax.ShapeDtypeStruct(r.shape, r.dtype) for r in results),
        in_specs=[hbm] * 3,
        out_specs=(hbm,) * 3,
        scratch_shapes=[pltpu.VMEM(r.shape, r.dtype) for r in results] + [sem((3,)), sem((3,))],
        compiler_params=pltpu.CompilerParams(vmem_limit_bytes=56 * 1024 * 1024),
    )(*results)
    return (token_loss.reshape(TOK), input_grad, table_grad[None])


def solution(mesh):
    return jax.shard_map(
        body,
        mesh=mesh,
        in_specs=(
            P("dp", None),
            P("vocab", None),
            P("dp"),
            P("dp"),
            P(("dp", "vocab")),
            P(("dp", "vocab"), None),
        ),
        out_specs=(P("dp"), P(("dp", "vocab"), None), P("vocab", "dp", None)),
        check_vma=False,
    )
```

```python
import functools
import math

import jax
import jax.numpy as jnp
from jax import lax
from jax.experimental import pallas as pl
from jax.experimental.pallas import tpu as pltpu
from jax.sharding import PartitionSpec as P

MESH = pl.DeviceIdType.MESH
SOFTCAP = 30.0
F32 = jnp.float32
BF16 = jnp.bfloat16

D = 4608
ENT = 96
TOK = 192
ROWS = 24
QUARTER = D // 4
PAIR = 2 * ROWS
PART_A = 640
PART_B = QUARTER - PART_A
HALF = 1024
STEP = 384
NX, NY, NZ, NC = 4, 4, 32, 2


def nt(a, b):
    return lax.dot_general(a, b, (((1,), (1,)), ((), ())), preferred_element_type=F32)


def tn(a, b):
    return lax.dot_general(a, b, (((0,), (0,)), ((), ())), preferred_element_type=F32)


def nn(a, b):
    return jnp.dot(a, b, preferred_element_type=F32)


def kernel(
    hidden_hbm, table_hbm, embed_hbm, targets_hbm, weight_hbm, ids_hbm,
    loss_hbm, input_hbm, table_grad_hbm,
    hid, tab, emb_in, targets_ref, weight_ref, ids_ref, loss_ref, input_ref, table_grad_ref, emb_a, emb_b, stats, xs, xown, xr, acc, ig_core, ig_core_in, ig_own, ig_y, ig_y_in,
    units, zf, zs, zr1, bf, bs, br1, b2f, b2, b2r, zb, zm, zr2,
    load_sem, out_sem, in2_sem, in4_sem, in8_sem, emb_s, emb_r, fwd_s, fwd_r, st_s, st_r, x_s, x_r, c_s, c_r, y_s, y_r, z1_s, z1_r, b1_s, b1_r, b2_s, b2_r, z2_s, z2_r,
):
    dp = lax.axis_index("dp")
    vocab = lax.axis_index("vocab")
    z, x = dp // NX, lax.rem(dp, NX)
    y, core = vocab // NC, lax.rem(vocab, NC)
    slot = core * NY + y

    def at(dz=0, dx=0, dy=0, dc=0):
        zz, xx = lax.rem(z + dz + NZ, NZ), lax.rem(x + dx + NX, NX)
        yy, cc = lax.rem(y + dy + NY, NY), lax.rem(core + dc, NC)
        return (zz * NX + xx, yy * NC + cc)

    def remote(src, dst, send, recv, device):
        return pltpu.make_async_remote_copy(
            src_ref=src, dst_ref=dst, send_sem=send, recv_sem=recv, device_id=device, device_id_type=MESH
        )

    loads = [
        pltpu.make_async_copy(embed_hbm, emb_in, load_sem.at[0]),
        pltpu.make_async_copy(table_hbm, tab, load_sem.at[1]),
        pltpu.make_async_copy(hidden_hbm, hid, load_sem.at[2]),
        pltpu.make_async_copy(targets_hbm, targets_ref, load_sem.at[3]),
        pltpu.make_async_copy(weight_hbm, weight_ref, load_sem.at[4]),
        pltpu.make_async_copy(ids_hbm, ids_ref, load_sem.at[5]),
    ]
    for load in loads:
        load.start()

    two = 2 - 4 * core
    near = (two, 1, -1)
    far = (4, 3, 5, 2, 6, 1, 7)
    group = [(dy, dc) for dy in (2, 1, 3, 0) for dc in range(NC) if (dy, dc) != (0, 0)]
    greeted = [at(dy=dy, dc=dc) for dy, dc in group]
    greeted += [at(dx=dx) for dx in (2, 1, 3)]
    greeted += [at(dz=dz) for dz in (1, -1, 2, -2)]
    barrier = pltpu.get_barrier_semaphore()
    for device in greeted:
        pl.semaphore_signal(barrier, inc=1, device_id=device, device_id_type=MESH)

    loads[0].wait()
    row = lax.broadcasted_iota(jnp.int32, (PAIR, ROWS), 0)
    col = lax.broadcasted_iota(jnp.int32, (PAIR, ROWS), 1)
    upper = (row == col).astype(BF16)
    lower = (row == col + ROWS).astype(BF16)
    for p in range(2):
        for lo, hi, dst in ((0, 384, emb_a), (384, PART_A, emb_a), (PART_A, QUARTER, emb_b)):
            left = 2 * p * QUARTER
            placed = nn(upper, emb_in[:, left + lo : left + hi]) + nn(
                lower, emb_in[:, left + QUARTER + lo : left + QUARTER + hi]
            )
            base = 0 if dst is emb_a else PART_A
            dst[p, slot, :, lo - base : hi - base] = placed.astype(BF16)

    pl.semaphore_wait(barrier, len(greeted))

    def pass_on(reach, heard):
        for dz in (reach, -reach):
            pl.semaphore_signal(heard, inc=1, device_id=at(dz=dz), device_id_type=MESH)

    emb_copies = []

    pieces = ((emb_a, 0), (emb_b, 0), (emb_a, 1), (emb_b, 1))

    def send_rows(n):
        rows, p = pieces[n]
        for dy in (2, 1, 3):
            copy = remote(
                rows.at[p, slot], rows.at[p, slot], emb_s.at[n, dy - 1], emb_r.at[n, dy - 1], at(dy=dy)
            )
            copy.start()
            emb_copies.append(copy)

    send_rows(0)
    pass_on(2, in2_sem)

    loads[1].wait()
    for load in loads[2:]:
        load.wait()
    squashed = jnp.tanh(nt(tab[...], hid[...]) / SOFTCAP)
    capped = SOFTCAP * squashed
    exponent = jnp.exp(capped)
    entry = lax.broadcasted_iota(jnp.int32, (ENT, TOK), 0) + vocab * ENT
    hit = entry == targets_ref[...]

    lane = lax.broadcasted_iota(jnp.int32, (1, 8 * PAIR), 1)
    place = lane - slot * PAIR
    ids_row = jnp.zeros((1, 8 * PAIR), F32)
    for r in range(ROWS):
        ids_row = jnp.where((place == r) | (place == r + ROWS), ids_ref[r].astype(F32), ids_row)
    stats[slot] = jnp.zeros((8, 8 * PAIR), F32)
    stats[slot, 0:1, 0:TOK] = jnp.sum(exponent, axis=0, keepdims=True)
    stats[slot, 1:2, 0:TOK] = jnp.sum(jnp.where(hit, capped, 0.0), axis=0, keepdims=True)
    stats[slot, 2:3, :] = ids_row
    st_copies = []
    for i, (dy, dc) in enumerate(group):
        copy = remote(stats.at[slot], stats.at[slot], st_s.at[i], st_r.at[i], at(dy=dy, dc=dc))
        copy.start()
        st_copies.append(copy)
    for n in (1, 2, 3):
        send_rows(n)
    pl.semaphore_wait(in2_sem, 2)
    pass_on(4, in4_sem)
    for copy in st_copies:
        copy.wait_recv()
    total = stats[0]
    for i in range(1, 8):
        total = total + stats[i]
    normalizer = total[0:1, 0:TOK]
    picked = total[1:2, 0:TOK]
    ids_all = total[2:3, :]
    loss_ref[...] = jnp.log(normalizer) - picked
    loss_out = pltpu.make_async_copy(loss_ref, loss_hbm, out_sem.at[0])
    loss_out.start()
    dlogit = (
        weight_ref[...] * (exponent / normalizer - hit.astype(F32)) * (1.0 - squashed * squashed)
    ).astype(BF16)

    def named(shape):
        i = lax.broadcasted_iota(jnp.int32, shape, 0)
        third, inner = i // 32, lax.rem(i, 32)
        cls, k = inner // 8, lax.rem(inner, 8)
        return 3 * (4 * k + cls) + third

    order = (named((ENT, ENT)) == lax.broadcasted_iota(jnp.int32, (ENT, ENT), 1)).astype(BF16)
    ordered = nn(order, dlogit).astype(BF16)
    named_id = (named((ENT, 8 * PAIR)) + vocab * ENT).astype(F32)
    is_lower = lax.rem(lax.broadcasted_iota(jnp.int32, (ENT, 8 * PAIR), 1), PAIR) >= ROWS
    match = named_id == ids_all
    wanted = [
        (match & jnp.logical_not(is_lower)).astype(BF16),
        (match & is_lower).astype(BF16),
    ]

    def forward(n):
        rows, p = pieces[n]
        mine = rows.at[p, pl.ds(core * NY, NY)]
        return remote(mine, mine, fwd_s.at[n], fwd_r.at[n], at(dc=1))

    scale = math.sqrt(D)
    x_copy = lambda to, j: remote(
        xs.at[to, j],
        xr.at[lax.rem(x - to + NX, NX) - 1, j],
        x_s.at[to, j],
        x_r.at[lax.rem(x - to + NX, NX) - 1, j],
        (z * NX + to, vocab),
    )
    fwd_copies = []
    b1_copies = []
    for n, (held, p) in enumerate(pieces):
        for copy in emb_copies[3 * n : 3 * n + 3]:
            copy.wait_recv()
        copy = forward(n)
        copy.start()
        fwd_copies.append(copy)
        copy.wait_recv()
        for h in range(2):
            q = 2 * p + h

            def product(lo, hi, base):
                rows = held[p, :, :, lo - base : hi - base].reshape(8 * PAIR, hi - lo)
                part = nn(ordered, hid[:, q * QUARTER + lo : q * QUARTER + hi])
                return part + scale * nn(wanted[h], rows)

            if held is emb_b:
                part = product(PART_A, QUARTER, PART_A)
                for r in range(3):
                    for c in range(4):
                        eight = part[32 * r + 8 * c : 32 * r + 8 * (c + 1)]
                        folded = jnp.concatenate([eight[:, : PART_B // 2], eight[:, PART_B // 2 :]], axis=0)
                        bf[c, p, 2 * r + h] = folded
                        bs[c, p, 2 * r + h] = folded.astype(BF16)
                continue
            for lo, hi in ((0, 384), (384, PART_A)):
                part = product(lo, hi, 0)
                for r in range(3):
                    to, j = divmod(4 * r + q, 3)
                    mine = part[32 * r : 32 * (r + 1)]
                    xs[to, j, :, lo:hi] = mine.astype(BF16)

                    @pl.when(x == to)
                    def _(mine=mine, j=j, lo=lo, hi=hi):
                        xown[j, :, lo:hi] = mine

            for r in range(3):
                to, j = divmod(4 * r + q, 3)

                @pl.when(x != to)
                def _(to=to, j=j):
                    x_copy(to, j).start()

        if held is emb_b:
            for i, dz in enumerate(near):
                copy = remote(
                    bs.at[lax.rem(z + dz + 4, 4), p], br1.at[i, p], b1_s.at[i, p], b1_r.at[i, p], at(dz=dz)
                )
                copy.start()
                b1_copies.append(copy)

    pl.semaphore_wait(in4_sem, 2)
    pass_on(8, in8_sem)

    for p in range(2):
        for s in range(QUARTER // STEP):
            left = p * 2 * QUARTER + s * STEP
            a = tn(dlogit, tab[:, left : left + STEP])
            b = tn(dlogit, tab[:, left + QUARTER : left + QUARTER + STEP])
            for v in range(8):
                take = slice(ROWS * v, ROWS * (v + 1))
                acc[p, v, :, s * STEP : (s + 1) * STEP] = jnp.concatenate([a[take], b[take]], axis=0)
    core_copies = []
    for p in range(2):
        for to in range(NY):
            ig_core[p, to] = acc[p, 2 * to + 1 - core].astype(BF16)
        copy = remote(ig_core.at[p], ig_core_in.at[p], c_s.at[p], c_r.at[p], at(dc=1))
        copy.start()
        core_copies.append(copy)

    for j in range(3):
        for d in range(3):
            remote(xs.at[0, j], xr.at[d, j], x_s.at[0, j], x_r.at[d, j], at(dx=1)).wait_recv()
        units[j] = (
            xown[j] + xr[0, j].astype(F32) + xr[1, j].astype(F32) + xr[2, j].astype(F32)
        )
    for c in range(4):
        rows = slice(8 * c, 8 * (c + 1))
        zf[c, 0:8, 0:640] = units[0, rows, :]
        zf[c, 0:8, 640:1024] = units[1, rows, 0:384]
        zf[c, 8:16, 0:256] = units[1, rows, 384:640]
        zf[c, 8:16, 256:896] = units[2, rows, :]
        zf[c, 8:16, 896:1024] = jnp.zeros((8, 128), F32)
        zs[c] = zf[c].astype(BF16)
    z1_copies = []
    for i, dz in enumerate(near):
        copy = remote(
            zs.at[lax.rem(z + dz + 4, 4)], zr1.at[i], z1_s.at[i], z1_r.at[i], at(dz=dz)
        )
        copy.start()
        z1_copies.append(copy)

    for copy in b1_copies:
        copy.wait_recv()
    for p in range(2):
        for i in range(6):
            r, h = divmod(i, 2)
            to, j = divmod(4 * r + 2 * p + h, 3)
            four = bf[lax.rem(z, 4), p, i]
            for n in range(3):
                four = four + br1[n, p, i].astype(F32)
            b2f[to, j] = four
            b2[to, j] = four.astype(BF16)
    b2_copies = []
    for i, dx in enumerate((1, 2, 3)):
        copy = remote(b2.at[lax.rem(x + dx, NX)], b2r.at[i], b2_s.at[i], b2_r.at[i], at(dx=dx))
        copy.start()
        b2_copies.append(copy)

    y_copies = []
    for p in range(2):
        core_copies[p].wait_recv()
        for dy in (2, 1, 3, 0):
            to = lax.rem(y + dy, NY)
            both = acc[p, 2 * to + core] + ig_core_in[p, to].astype(F32)
            if dy == 0:
                ig_own[p] = both
            else:
                ig_y[p, dy - 1] = both.astype(BF16)
                copy = remote(
                    ig_y.at[p, dy - 1], ig_y_in.at[p, dy - 1], y_s.at[p, dy - 1], y_r.at[p, dy - 1], at(dy=dy)
                )
                copy.start()
                y_copies.append(copy)

    for copy in z1_copies + b2_copies:
        copy.wait_recv()
    part = (
        zf[lax.rem(z, 4)] + zr1[0].astype(F32) + zr1[1].astype(F32) + zr1[2].astype(F32)
    )
    zb[...] = jnp.zeros_like(zb)
    for j in range(3):
        lower_part = b2f[x, j]
        for n in range(3):
            lower_part = lower_part + b2r[n, j].astype(F32)
        for line in range(5):
            up, at_line = divmod(5 * j + line, 8)
            zb[:, 9 * j + line, :] = part[8 * up : 8 * (up + 1), 128 * at_line : 128 * (at_line + 1)]
        for line in range(4):
            up, at_line = divmod(line, 2)
            zb[:, 9 * j + 5 + line, :] = lower_part[8 * up : 8 * (up + 1), 128 * at_line : 128 * (at_line + 1)]
    zm[...] = zb[...].astype(BF16)
    pl.semaphore_wait(in8_sem, 2)
    z2_copies = []
    for d in far:
        copy = remote(
            zm.at[lax.rem(z // 4 + d, 8)], zr2.at[d - 1], z2_s.at[d - 1], z2_r.at[d - 1], at(dz=4 * d)
        )
        copy.start()
        z2_copies.append(copy)

    for copy in y_copies:
        copy.wait_recv()
    for p in range(2):
        whole = ig_own[p]
        for i in range(3):
            whole = whole + ig_y_in[p, i].astype(F32)
        input_ref[:, p * 2 * QUARTER : p * 2 * QUARTER + QUARTER] = whole[:ROWS].astype(BF16)
        input_ref[:, p * 2 * QUARTER + QUARTER : (p + 1) * 2 * QUARTER] = whole[ROWS:].astype(BF16)
    input_out = pltpu.make_async_copy(input_ref, input_hbm, out_sem.at[1])
    input_out.start()

    for copy in emb_copies + fwd_copies + st_copies + core_copies + y_copies + z1_copies + b1_copies + b2_copies:
        copy.wait_send()
    for to in range(NX):
        for j in range(3):

            @pl.when(x != to)
            def _(to=to, j=j):
                x_copy(to, j).wait_send()

    for copy in z2_copies:
        copy.wait_recv()
    lines = zb[z // 4]
    for i in range(7):
        lines = lines + zr2[i].astype(F32)
    table_grad_ref[...] = lines[:27].astype(BF16)
    table_out = pltpu.make_async_copy(table_grad_ref, table_grad_hbm, out_sem.at[2])
    table_out.start()
    for copy in z2_copies:
        copy.wait_send()
    for copy in (loss_out, input_out, table_out):
        copy.wait()


def hand_over(a, b, c, a_out, b_out, c_out, a_mid, b_mid, c_mid, in_sem, out_sem):
    arrive = [
        pltpu.make_async_copy(src, mid, in_sem.at[i])
        for i, (src, mid) in enumerate(((a, a_mid), (b, b_mid), (c, c_mid)))
    ]
    leave = [
        pltpu.make_async_copy(mid, dst, out_sem.at[i])
        for i, (mid, dst) in enumerate(((a_mid, a_out), (b_mid, b_out), (c_mid, c_out)))
    ]
    for copy in arrive:
        copy.start()
    for come, go in zip(arrive, leave):
        come.wait()
        go.start()
    for copy in leave:
        copy.wait()


def body(hidden, table, targets, loss_weight, token_ids, grad_embed):
    hbm = pl.BlockSpec(memory_space=pl.ANY)
    sem = pltpu.SemaphoreType.DMA
    results = pl.pallas_call(
        kernel,
        out_shape=(
            jax.ShapeDtypeStruct((1, TOK), F32),
            jax.ShapeDtypeStruct((ROWS, D), BF16),
            jax.ShapeDtypeStruct((27, 128), BF16),
        ),
        in_specs=[hbm] * 6,
        out_specs=(hbm,) * 3,
        scratch_shapes=[
            pltpu.VMEM((TOK, D), BF16),
            pltpu.VMEM((ENT, D), BF16),
            pltpu.VMEM((ROWS, D), BF16),
            pltpu.VMEM((1, TOK), jnp.int32),
            pltpu.VMEM((1, TOK), F32),
            pltpu.SMEM((ROWS,), jnp.int32),
            pltpu.VMEM((1, TOK), F32),
            pltpu.VMEM((ROWS, D), BF16),
            pltpu.VMEM((27, 128), BF16),
            pltpu.VMEM((2, 8, PAIR, PART_A), BF16),
            pltpu.VMEM((2, 8, PAIR, PART_B), BF16),
            pltpu.VMEM((8, 8, 8 * PAIR), F32),
            pltpu.VMEM((NX, 3, 32, PART_A), BF16),
            pltpu.VMEM((3, 32, PART_A), F32),
            pltpu.VMEM((3, 3, 32, PART_A), BF16),
            pltpu.VMEM((2, 8, PAIR, QUARTER), F32),
            pltpu.VMEM((2, NY, PAIR, QUARTER), BF16),
            pltpu.VMEM((2, NY, PAIR, QUARTER), BF16),
            pltpu.VMEM((2, PAIR, QUARTER), F32),
            pltpu.VMEM((2, 3, PAIR, QUARTER), BF16),
            pltpu.VMEM((2, 3, PAIR, QUARTER), BF16),
            pltpu.VMEM((3, 32, PART_A), F32),
            pltpu.VMEM((4, 16, HALF), F32),
            pltpu.VMEM((4, 16, HALF), BF16),
            pltpu.VMEM((3, 16, HALF), BF16),
            pltpu.VMEM((4, 2, 6, 16, PART_B // 2), F32),
            pltpu.VMEM((4, 2, 6, 16, PART_B // 2), BF16),
            pltpu.VMEM((3, 2, 6, 16, PART_B // 2), BF16),
            pltpu.VMEM((NX, 3, 16, PART_B // 2), F32),
            pltpu.VMEM((NX, 3, 16, PART_B // 2), BF16),
            pltpu.VMEM((3, 3, 16, PART_B // 2), BF16),
            pltpu.VMEM((8, 32, 128), F32),
            pltpu.VMEM((8, 32, 128), BF16),
            pltpu.VMEM((7, 32, 128), BF16),
            sem((6,)), sem((3,)),
            pltpu.SemaphoreType.REGULAR, pltpu.SemaphoreType.REGULAR, pltpu.SemaphoreType.REGULAR,
            sem((4, 3)), sem((4, 3)),
            sem((4,)), sem((4,)),
            sem((7,)), sem((7,)),
            sem((NX, 3)), sem((3, 3)),
            sem((2,)), sem((2,)),
            sem((2, 3)), sem((2, 3)),
            sem((3,)), sem((3,)),
            sem((3, 2)), sem((3, 2)),
            sem((3,)), sem((3,)),
            sem((7,)), sem((7,)),
        ],
        compiler_params=pltpu.CompilerParams(
            collective_id=0, has_side_effects=True, vmem_limit_bytes=56 * 1024 * 1024
        ),
    )(hidden, table, grad_embed, targets.reshape(1, TOK), loss_weight.reshape(1, TOK), token_ids)
    token_loss, input_grad, table_grad = pl.pallas_call(
        hand_over,
        out_shape=tuple(jax.ShapeDtypeStruct(r.shape, r.dtype) for r in results),
        in_specs=[hbm] * 3,
        out_specs=(hbm,) * 3,
        scratch_shapes=[pltpu.VMEM(r.shape, r.dtype) for r in results] + [sem((3,)), sem((3,))],
        compiler_params=pltpu.CompilerParams(vmem_limit_bytes=56 * 1024 * 1024),
    )(*results)
    return (token_loss.reshape(TOK), input_grad, table_grad[None])


def solution(mesh):
    return jax.shard_map(
        body,
        mesh=mesh,
        in_specs=(
            P("dp", None),
            P("vocab", None),
            P("dp"),
            P("dp"),
            P(("dp", "vocab")),
            P(("dp", "vocab"), None),
        ),
        out_specs=(P("dp"), P(("dp", "vocab"), None), P("vocab", "dp", None)),
        check_vma=False,
    )
```

```python
import functools
import math

import jax
import jax.numpy as jnp
from jax import lax
from jax.experimental import pallas as pl
from jax.experimental.pallas import tpu as pltpu
from jax.sharding import PartitionSpec as P

MESH = pl.DeviceIdType.MESH
SOFTCAP = 30.0
F32 = jnp.float32
BF16 = jnp.bfloat16

D = 4608
ENT = 96
TOK = 192
ROWS = 24
QUARTER = D // 4
PAIR = 2 * ROWS
PART_A = 640
PART_B = QUARTER - PART_A
HALF = 1024
STEP = 384
NX, NY, NZ, NC = 4, 4, 32, 2


def nt(a, b):
    return lax.dot_general(a, b, (((1,), (1,)), ((), ())), preferred_element_type=F32)


def tn(a, b):
    return lax.dot_general(a, b, (((0,), (0,)), ((), ())), preferred_element_type=F32)


def nn(a, b):
    return jnp.dot(a, b, preferred_element_type=F32)


def kernel(
    hidden_hbm, table_hbm, embed_hbm, targets_hbm, weight_hbm, ids_hbm,
    loss_hbm, input_hbm, table_grad_hbm,
    hid, tab, emb_in, targets_ref, weight_ref, ids_ref, loss_ref, input_ref, table_grad_ref, emb_a, emb_b, stats, xs, xown, xr, acc, ig_core, ig_core_in, ig_own, ig_y, ig_y_in,
    units, zf, zs, zr1, bf, bs, br1, b2f, b2, b2r, zb, zm, zr2,
    load_sem, out_sem, in2_sem, in4_sem, in8_sem, emb_s, emb_r, fwd_s, fwd_r, st_s, st_r, x_s, x_r, c_s, c_r, y_s, y_r, z1_s, z1_r, b1_s, b1_r, b2_s, b2_r, z2_s, z2_r,
):
    dp = lax.axis_index("dp")
    vocab = lax.axis_index("vocab")
    z, x = dp // NX, lax.rem(dp, NX)
    y, core = vocab // NC, lax.rem(vocab, NC)
    slot = core * NY + y

    def at(dz=0, dx=0, dy=0, dc=0):
        zz, xx = lax.rem(z + dz + NZ, NZ), lax.rem(x + dx + NX, NX)
        yy, cc = lax.rem(y + dy + NY, NY), lax.rem(core + dc, NC)
        return (zz * NX + xx, yy * NC + cc)

    def remote(src, dst, send, recv, device):
        return pltpu.make_async_remote_copy(
            src_ref=src, dst_ref=dst, send_sem=send, recv_sem=recv, device_id=device, device_id_type=MESH
        )

    loads = [
        pltpu.make_async_copy(embed_hbm, emb_in, load_sem.at[0]),
        pltpu.make_async_copy(table_hbm, tab, load_sem.at[1]),
        pltpu.make_async_copy(hidden_hbm, hid, load_sem.at[2]),
        pltpu.make_async_copy(targets_hbm, targets_ref, load_sem.at[3]),
        pltpu.make_async_copy(weight_hbm, weight_ref, load_sem.at[4]),
        pltpu.make_async_copy(ids_hbm, ids_ref, load_sem.at[5]),
    ]
    for load in loads:
        load.start()

    two = 2 - 4 * core
    near = (two, 1, -1)
    far = (4, 3, 5, 2, 6, 1, 7)
    group = [(dy, dc) for dy in (2, 1, 3, 0) for dc in range(NC) if (dy, dc) != (0, 0)]
    greeted = [at(dy=dy, dc=dc) for dy, dc in group]
    greeted += [at(dx=dx) for dx in (2, 1, 3)]
    greeted += [at(dz=dz) for dz in (1, -1, 2, -2)]
    barrier = pltpu.get_barrier_semaphore()
    for device in greeted:
        pl.semaphore_signal(barrier, inc=1, device_id=device, device_id_type=MESH)

    loads[0].wait()
    row = lax.broadcasted_iota(jnp.int32, (PAIR, ROWS), 0)
    col = lax.broadcasted_iota(jnp.int32, (PAIR, ROWS), 1)
    upper = (row == col).astype(BF16)
    lower = (row == col + ROWS).astype(BF16)
    for p in range(2):
        for lo, hi, dst in ((0, 384, emb_a), (384, PART_A, emb_a), (PART_A, QUARTER, emb_b)):
            left = 2 * p * QUARTER
            placed = nn(upper, emb_in[:, left + lo : left + hi]) + nn(
                lower, emb_in[:, left + QUARTER + lo : left + QUARTER + hi]
            )
            base = 0 if dst is emb_a else PART_A
            dst[p, slot, :, lo - base : hi - base] = placed.astype(BF16)

    pl.semaphore_wait(barrier, len(greeted))

    def pass_on(reach, heard):
        for dz in (reach, -reach):
            pl.semaphore_signal(heard, inc=1, device_id=at(dz=dz), device_id_type=MESH)

    emb_copies = []

    pieces = ((emb_a, 0), (emb_b, 0), (emb_a, 1), (emb_b, 1))

    def send_rows(n):
        rows, p = pieces[n]
        for dy in (2, 1, 3):
            copy = remote(
                rows.at[p, slot], rows.at[p, slot], emb_s.at[n, dy - 1], emb_r.at[n, dy - 1], at(dy=dy)
            )
            copy.start()
            emb_copies.append(copy)

    send_rows(0)
    pass_on(2, in2_sem)

    loads[1].wait()
    for load in loads[2:]:
        load.wait()
    squashed = jnp.tanh(nt(tab[...], hid[...]) / SOFTCAP)
    capped = SOFTCAP * squashed
    exponent = jnp.exp(capped)
    entry = lax.broadcasted_iota(jnp.int32, (ENT, TOK), 0) + vocab * ENT
    hit = entry == targets_ref[...]

    lane = lax.broadcasted_iota(jnp.int32, (1, 8 * PAIR), 1)
    place = lane - slot * PAIR
    ids_row = jnp.zeros((1, 8 * PAIR), F32)
    for r in range(ROWS):
        ids_row = jnp.where((place == r) | (place == r + ROWS), ids_ref[r].astype(F32), ids_row)
    stats[slot] = jnp.zeros((1, 896), F32)
    stats[slot, :, 0:TOK] = jnp.sum(exponent, axis=0, keepdims=True)
    stats[slot, :, 256 : 256 + TOK] = jnp.sum(jnp.where(hit, capped, 0.0), axis=0, keepdims=True)
    stats[slot, :, 512:896] = ids_row
    st_copies = []
    for i, (dy, dc) in enumerate(group):
        copy = remote(stats.at[slot], stats.at[slot], st_s.at[i], st_r.at[i], at(dy=dy, dc=dc))
        copy.start()
        st_copies.append(copy)
    for n in (1, 2, 3):
        send_rows(n)
    pl.semaphore_wait(in2_sem, 2)
    pass_on(4, in4_sem)
    for copy in st_copies:
        copy.wait_recv()
    total = stats[0]
    for i in range(1, 8):
        total = total + stats[i]
    normalizer = total[:, 0:TOK]
    picked = total[:, 256 : 256 + TOK]
    ids_all = total[:, 512:896]
    loss_ref[...] = jnp.log(normalizer) - picked
    loss_out = pltpu.make_async_copy(loss_ref, loss_hbm, out_sem.at[0])
    loss_out.start()
    dlogit = (
        weight_ref[...] * (exponent / normalizer - hit.astype(F32)) * (1.0 - squashed * squashed)
    ).astype(BF16)

    def named(shape):
        i = lax.broadcasted_iota(jnp.int32, shape, 0)
        third, inner = i // 32, lax.rem(i, 32)
        cls, k = inner // 8, lax.rem(inner, 8)
        return 3 * (4 * k + cls) + third

    order = (named((ENT, ENT)) == lax.broadcasted_iota(jnp.int32, (ENT, ENT), 1)).astype(BF16)
    ordered = nn(order, dlogit).astype(BF16)
    named_id = (named((ENT, 8 * PAIR)) + vocab * ENT).astype(F32)
    is_lower = lax.rem(lax.broadcasted_iota(jnp.int32, (ENT, 8 * PAIR), 1), PAIR) >= ROWS
    match = named_id == ids_all
    wanted = [
        (match & jnp.logical_not(is_lower)).astype(BF16),
        (match & is_lower).astype(BF16),
    ]

    def forward(n):
        rows, p = pieces[n]
        mine = rows.at[p, pl.ds(core * NY, NY)]
        return remote(mine, mine, fwd_s.at[n], fwd_r.at[n], at(dc=1))

    scale = math.sqrt(D)
    x_copy = lambda to, j: remote(
        xs.at[to, j],
        xr.at[lax.rem(x - to + NX, NX) - 1, j],
        x_s.at[to, j],
        x_r.at[lax.rem(x - to + NX, NX) - 1, j],
        (z * NX + to, vocab),
    )
    fwd_copies = []
    b1_copies = []
    for n, (held, p) in enumerate(pieces):
        for copy in emb_copies[3 * n : 3 * n + 3]:
            copy.wait_recv()
        copy = forward(n)
        copy.start()
        fwd_copies.append(copy)
        copy.wait_recv()
        for h in range(2):
            q = 2 * p + h

            def product(lo, hi, base):
                rows = held[p, :, :, lo - base : hi - base].reshape(8 * PAIR, hi - lo)
                part = nn(ordered, hid[:, q * QUARTER + lo : q * QUARTER + hi])
                return part + scale * nn(wanted[h], rows)

            if held is emb_b:
                part = product(PART_A, QUARTER, PART_A)
                for r in range(3):
                    for c in range(4):
                        eight = part[32 * r + 8 * c : 32 * r + 8 * (c + 1)]
                        folded = jnp.concatenate([eight[:, : PART_B // 2], eight[:, PART_B // 2 :]], axis=0)
                        bf[c, p, 2 * r + h] = folded
                        bs[c, p, 2 * r + h] = folded.astype(BF16)
                continue
            for lo, hi in ((0, 384), (384, PART_A)):
                part = product(lo, hi, 0)
                for r in range(3):
                    to, j = divmod(4 * r + q, 3)
                    mine = part[32 * r : 32 * (r + 1)]
                    xs[to, j, :, lo:hi] = mine.astype(BF16)

                    @pl.when(x == to)
                    def _(mine=mine, j=j, lo=lo, hi=hi):
                        xown[j, :, lo:hi] = mine

            for r in range(3):
                to, j = divmod(4 * r + q, 3)

                @pl.when(x != to)
                def _(to=to, j=j):
                    x_copy(to, j).start()

        if held is emb_b:
            for i, dz in enumerate(near):
                copy = remote(
                    bs.at[lax.rem(z + dz + 4, 4), p], br1.at[i, p], b1_s.at[i, p], b1_r.at[i, p], at(dz=dz)
                )
                copy.start()
                b1_copies.append(copy)

    pl.semaphore_wait(in4_sem, 2)
    pass_on(8, in8_sem)

    for p in range(2):
        for s in range(QUARTER // STEP):
            left = p * 2 * QUARTER + s * STEP
            a = tn(dlogit, tab[:, left : left + STEP])
            b = tn(dlogit, tab[:, left + QUARTER : left + QUARTER + STEP])
            for v in range(8):
                take = slice(ROWS * v, ROWS * (v + 1))
                acc[p, v, :, s * STEP : (s + 1) * STEP] = jnp.concatenate([a[take], b[take]], axis=0)
    core_copies = []
    for p in range(2):
        for to in range(NY):
            ig_core[p, to] = acc[p, 2 * to + 1 - core].astype(BF16)
        copy = remote(ig_core.at[p], ig_core_in.at[p], c_s.at[p], c_r.at[p], at(dc=1))
        copy.start()
        core_copies.append(copy)

    for j in range(3):
        for d in range(3):
            remote(xs.at[0, j], xr.at[d, j], x_s.at[0, j], x_r.at[d, j], at(dx=1)).wait_recv()
        units[j] = (
            xown[j] + xr[0, j].astype(F32) + xr[1, j].astype(F32) + xr[2, j].astype(F32)
        )
    for c in range(4):
        rows = slice(8 * c, 8 * (c + 1))
        zf[c, 0:8, 0:640] = units[0, rows, :]
        zf[c, 0:8, 640:1024] = units[1, rows, 0:384]
        zf[c, 8:16, 0:256] = units[1, rows, 384:640]
        zf[c, 8:16, 256:896] = units[2, rows, :]
        zf[c, 8:16, 896:1024] = jnp.zeros((8, 128), F32)
        zs[c] = zf[c].astype(BF16)
    z1_copies = []
    for i, dz in enumerate(near):
        copy = remote(
            zs.at[lax.rem(z + dz + 4, 4)], zr1.at[i], z1_s.at[i], z1_r.at[i], at(dz=dz)
        )
        copy.start()
        z1_copies.append(copy)

    for copy in b1_copies:
        copy.wait_recv()
    for p in range(2):
        for i in range(6):
            r, h = divmod(i, 2)
            to, j = divmod(4 * r + 2 * p + h, 3)
            four = bf[lax.rem(z, 4), p, i]
            for n in range(3):
                four = four + br1[n, p, i].astype(F32)
            b2f[to, j] = four
            b2[to, j] = four.astype(BF16)
    b2_copies = []
    for i, dx in enumerate((2, 1, 3)):
        copy = remote(b2.at[lax.rem(x + dx, NX)], b2r.at[i], b2_s.at[i], b2_r.at[i], at(dx=dx))
        copy.start()
        b2_copies.append(copy)

    y_copies = []
    for p in range(2):
        core_copies[p].wait_recv()
        for dy in (2, 1, 3, 0):
            to = lax.rem(y + dy, NY)
            both = acc[p, 2 * to + core] + ig_core_in[p, to].astype(F32)
            if dy == 0:
                ig_own[p] = both
            else:
                ig_y[p, dy - 1] = both.astype(BF16)
                copy = remote(
                    ig_y.at[p, dy - 1], ig_y_in.at[p, dy - 1], y_s.at[p, dy - 1], y_r.at[p, dy - 1], at(dy=dy)
                )
                copy.start()
                y_copies.append(copy)

    for copy in z1_copies + b2_copies:
        copy.wait_recv()
    part = (
        zf[lax.rem(z, 4)] + zr1[0].astype(F32) + zr1[1].astype(F32) + zr1[2].astype(F32)
    )
    zb[...] = jnp.zeros_like(zb)
    for j in range(3):
        lower_part = b2f[x, j]
        for n in range(3):
            lower_part = lower_part + b2r[n, j].astype(F32)
        for line in range(5):
            up, at_line = divmod(5 * j + line, 8)
            zb[:, 9 * j + line, :] = part[8 * up : 8 * (up + 1), 128 * at_line : 128 * (at_line + 1)]
        for line in range(4):
            up, at_line = divmod(line, 2)
            zb[:, 9 * j + 5 + line, :] = lower_part[8 * up : 8 * (up + 1), 128 * at_line : 128 * (at_line + 1)]
    zm[...] = zb[...].astype(BF16)
    pl.semaphore_wait(in8_sem, 2)
    z2_copies = []
    for d in far:
        copy = remote(
            zm.at[lax.rem(z // 4 + d, 8)], zr2.at[d - 1], z2_s.at[d - 1], z2_r.at[d - 1], at(dz=4 * d)
        )
        copy.start()
        z2_copies.append(copy)

    for copy in y_copies:
        copy.wait_recv()
    for p in range(2):
        whole = ig_own[p]
        for i in range(3):
            whole = whole + ig_y_in[p, i].astype(F32)
        input_ref[:, p * 2 * QUARTER : p * 2 * QUARTER + QUARTER] = whole[:ROWS].astype(BF16)
        input_ref[:, p * 2 * QUARTER + QUARTER : (p + 1) * 2 * QUARTER] = whole[ROWS:].astype(BF16)
    input_out = pltpu.make_async_copy(input_ref, input_hbm, out_sem.at[1])
    input_out.start()

    for copy in emb_copies + fwd_copies + st_copies + core_copies + y_copies + z1_copies + b1_copies + b2_copies:
        copy.wait_send()
    for to in range(NX):
        for j in range(3):

            @pl.when(x != to)
            def _(to=to, j=j):
                x_copy(to, j).wait_send()

    for copy in z2_copies:
        copy.wait_recv()
    lines = zb[z // 4]
    for i in range(7):
        lines = lines + zr2[i].astype(F32)
    table_grad_ref[...] = lines[:27].astype(BF16)
    table_out = pltpu.make_async_copy(table_grad_ref, table_grad_hbm, out_sem.at[2])
    table_out.start()
    for copy in z2_copies:
        copy.wait_send()
    for copy in (loss_out, input_out, table_out):
        copy.wait()


def hand_over(a, b, c, a_out, b_out, c_out, a_mid, b_mid, c_mid, in_sem, out_sem):
    arrive = [
        pltpu.make_async_copy(src, mid, in_sem.at[i])
        for i, (src, mid) in enumerate(((a, a_mid), (b, b_mid), (c, c_mid)))
    ]
    leave = [
        pltpu.make_async_copy(mid, dst, out_sem.at[i])
        for i, (mid, dst) in enumerate(((a_mid, a_out), (b_mid, b_out), (c_mid, c_out)))
    ]
    for copy in arrive:
        copy.start()
    for come, go in zip(arrive, leave):
        come.wait()
        go.start()
    for copy in leave:
        copy.wait()


def body(hidden, table, targets, loss_weight, token_ids, grad_embed):
    hbm = pl.BlockSpec(memory_space=pl.ANY)
    sem = pltpu.SemaphoreType.DMA
    results = pl.pallas_call(
        kernel,
        out_shape=(
            jax.ShapeDtypeStruct((1, TOK), F32),
            jax.ShapeDtypeStruct((ROWS, D), BF16),
            jax.ShapeDtypeStruct((27, 128), BF16),
        ),
        in_specs=[hbm] * 6,
        out_specs=(hbm,) * 3,
        scratch_shapes=[
            pltpu.VMEM((TOK, D), BF16),
            pltpu.VMEM((ENT, D), BF16),
            pltpu.VMEM((ROWS, D), BF16),
            pltpu.VMEM((1, TOK), jnp.int32),
            pltpu.VMEM((1, TOK), F32),
            pltpu.SMEM((ROWS,), jnp.int32),
            pltpu.VMEM((1, TOK), F32),
            pltpu.VMEM((ROWS, D), BF16),
            pltpu.VMEM((27, 128), BF16),
            pltpu.VMEM((2, 8, PAIR, PART_A), BF16),
            pltpu.VMEM((2, 8, PAIR, PART_B), BF16),
            pltpu.VMEM((8, 1, 896), F32),
            pltpu.VMEM((NX, 3, 32, PART_A), BF16),
            pltpu.VMEM((3, 32, PART_A), F32),
            pltpu.VMEM((3, 3, 32, PART_A), BF16),
            pltpu.VMEM((2, 8, PAIR, QUARTER), F32),
            pltpu.VMEM((2, NY, PAIR, QUARTER), BF16),
            pltpu.VMEM((2, NY, PAIR, QUARTER), BF16),
            pltpu.VMEM((2, PAIR, QUARTER), F32),
            pltpu.VMEM((2, 3, PAIR, QUARTER), BF16),
            pltpu.VMEM((2, 3, PAIR, QUARTER), BF16),
            pltpu.VMEM((3, 32, PART_A), F32),
            pltpu.VMEM((4, 16, HALF), F32),
            pltpu.VMEM((4, 16, HALF), BF16),
            pltpu.VMEM((3, 16, HALF), BF16),
            pltpu.VMEM((4, 2, 6, 16, PART_B // 2), F32),
            pltpu.VMEM((4, 2, 6, 16, PART_B // 2), BF16),
            pltpu.VMEM((3, 2, 6, 16, PART_B // 2), BF16),
            pltpu.VMEM((NX, 3, 16, PART_B // 2), F32),
            pltpu.VMEM((NX, 3, 16, PART_B // 2), BF16),
            pltpu.VMEM((3, 3, 16, PART_B // 2), BF16),
            pltpu.VMEM((8, 32, 128), F32),
            pltpu.VMEM((8, 32, 128), BF16),
            pltpu.VMEM((7, 32, 128), BF16),
            sem((6,)), sem((3,)),
            pltpu.SemaphoreType.REGULAR, pltpu.SemaphoreType.REGULAR, pltpu.SemaphoreType.REGULAR,
            sem((4, 3)), sem((4, 3)),
            sem((4,)), sem((4,)),
            sem((7,)), sem((7,)),
            sem((NX, 3)), sem((3, 3)),
            sem((2,)), sem((2,)),
            sem((2, 3)), sem((2, 3)),
            sem((3,)), sem((3,)),
            sem((3, 2)), sem((3, 2)),
            sem((3,)), sem((3,)),
            sem((7,)), sem((7,)),
        ],
        compiler_params=pltpu.CompilerParams(
            collective_id=0, has_side_effects=True, vmem_limit_bytes=56 * 1024 * 1024
        ),
    )(hidden, table, grad_embed, targets.reshape(1, TOK), loss_weight.reshape(1, TOK), token_ids)
    token_loss, input_grad, table_grad = pl.pallas_call(
        hand_over,
        out_shape=tuple(jax.ShapeDtypeStruct(r.shape, r.dtype) for r in results),
        in_specs=[hbm] * 3,
        out_specs=(hbm,) * 3,
        scratch_shapes=[pltpu.VMEM(r.shape, r.dtype) for r in results] + [sem((3,)), sem((3,))],
        compiler_params=pltpu.CompilerParams(vmem_limit_bytes=56 * 1024 * 1024),
    )(*results)
    return (token_loss.reshape(TOK), input_grad, table_grad[None])


def solution(mesh):
    return jax.shard_map(
        body,
        mesh=mesh,
        in_specs=(
            P("dp", None),
            P("vocab", None),
            P("dp"),
            P("dp"),
            P(("dp", "vocab")),
            P(("dp", "vocab"), None),
        ),
        out_specs=(P("dp"), P(("dp", "vocab"), None), P("vocab", "dp", None)),
        check_vma=False,
    )
```
